256 devices in a mesh: rep: 2 (over core), ep: 128 (over x, z, y).
Axes of the slice: x: 4, y: 4, z: 8, core: 2. Of those that a mesh axis runs over, the one named last changes fastest.
Arguments:
- first_half: bfloat16 [16384, 2048], P('ep'), may hold values from -6 to 6
- second_half: bfloat16 [16384, 2048], P('ep'), may hold values from -6 to 6
- second_grad: bfloat16 [16384, 2048], P('ep'), may hold values from -3 to 3
- norm_gain: bfloat16 [2048], replicated, may hold values from 0.5 to 1.5
- expert_ids: int32 [16384, 8], P('ep'), may hold values from 0 to 127, all different within a row; in each aligned block of 128 rows (0 to 127, 128 to 255, ...) at most 10 rows name the same one
- gates: float32 [16384, 8], P('ep'), may hold values from 0.02 to 0.3
- w_gate: bfloat16 [128, 2048, 768], P('ep', None, 'rep'), may hold values from -0.125 to 0.125
- w_up: bfloat16 [128, 2048, 768], P('ep', None, 'rep'), may hold values from -0.125 to 0.125
- w_down: bfloat16 [128, 768, 2048], P('ep', 'rep'), may hold values from -0.21875 to 0.21875
Outputs:
- inverted: bfloat16 [16384, 2048], P('ep')
- first_grad: bfloat16 [16384, 2048], P('ep')
- gates_grad: float32 [16384, 8], P('ep')
- w_down_grad: bfloat16 [128, 768, 2048], P('ep', 'rep')
The draws below stay inside these ranges and needn't reach their ends.
Inputs may be any that keep to these rules, and one draw needn't show every extreme that they name: `expert_ids`: the 8 experts of a token are different. Among the tokens of one index of ep (aligned blocks of 128 rows) no expert is named by more than 10 tokens, and in every draw some expert is named by exactly 10 tokens of some block.
All inputs are finite; a program needn't handle non-finite values.
Results may differ from the reference program's by a relative error of at most 0.0072.
Values may be sent and summed in bfloat16 or wider, within the bound.
A program may use at most 128 MiB of HBM per device.

```python
import math
import jax
import jax.numpy as jnp
import numpy as np
from jax import lax

D = 2048
FF = 768
TOP = 8
TOK_DEV = 128
EXPERTS = 128
TOKENS = 16384
CAP = 10


def shard_levels(rng, dims, pieces, smallest, high):
    def one(dim, parts):
        steps = jax.random.uniform(jax.random.fold_in(jax.random.fold_in(rng, 6), dim), (parts,), jnp.float32, smallest / len(pieces), high / len(pieces))
        return jnp.repeat(jnp.exp(steps), dims[dim] // parts).reshape((-1,) + (1,) * (len(dims) - dim - 1))

    gain = one(*pieces[0])
    for cut in pieces[1:]:
        gain = gain * one(*cut)
    return gain


def routed_block(rng, own, number, rows, number_of, top, bound, lean):
    ranking = jax.random.permutation(rng, number_of)
    packed, ordinary = portions_of(number_of, rows * top, bound, lean, True), portions_of(number_of, rows * top, bound, lean, False)
    places = jnp.arange(number_of)

    def named(sizes, turn):
        used = int((sizes > 0).sum())
        fixed = max(1, used // 4)
        moved = fixed + (places - fixed + turn * (used - fixed)) % max(1, number_of - fixed)
        return jnp.zeros((number_of,), jnp.int32).at[ranking[jnp.where(places < fixed, places, moved)]].set(jnp.asarray(sizes, jnp.int32))

    sizes = jnp.where(number % 4 == 0, named(packed, number // 4), named(ordinary, number - number // 4 - 1))
    mixed = jax.random.permutation(jax.random.fold_in(own, 3), number_of)
    source_of, receiver = mixed[0:number_of // 2 * 2:2], mixed[1:number_of // 2 * 2:2]
    room = jnp.minimum(sizes[source_of] - 1, bound - sizes[receiver]) // 2
    room = jnp.where((source_of == ranking[0]) | (receiver == ranking[0]) | (sizes[receiver] == 0), 0, jnp.maximum(room, 0))
    moved = jax.random.randint(jax.random.fold_in(own, 4), (number_of // 2,), 0, 1 << 20) % (room + 1)
    sizes = sizes.at[source_of].add(-moved).at[receiver].add(moved)
    members = jnp.searchsorted(jnp.cumsum(sizes), jnp.arange(rows * top), side="right").astype(jnp.int32)
    listing = members.reshape(top, rows).T
    listing = listing[jax.random.permutation(jax.random.fold_in(own, 1), rows)]
    turn = jax.random.randint(jax.random.fold_in(own, 2), (rows, 1), 0, top)
    return jnp.take_along_axis(listing, (jnp.arange(top)[None, :] + turn) % top, axis=1)


def portions_of(amount, total, bound, lean, full):
    weights = [(1 << 20) // math.isqrt(standing ** lean) + 1 for standing in range(1, amount + 1)]
    largest = bound if full else min(bound, max(-(-total // amount), total * weights[0] // sum(weights)))
    least = 1 if total - largest >= amount - 1 else 0
    holding, surplus = [largest] + [least] * (amount - 1), total - largest - least * (amount - 1)
    while surplus > 0:
        movable = [i for i in range(1, amount) if holding[i] < largest] or [i for i in range(1, amount) if holding[i] < bound]
        pool, left = sum([weights[i] for i in movable]), surplus
        for i in movable:
            extra = min(bound - holding[i], max(1, left * weights[i] // pool), surplus)
            holding[i] = holding[i] + extra
            surplus = surplus - extra
    return np.array(holding)


def centred(rng, dims, deviation, most, pieces=(), held_as=jnp.bfloat16):
    loudness = shard_levels(rng, dims, pieces, -0.22, 0.18) if pieces else 1.0
    result = jax.random.normal(rng, dims, jnp.float32) * deviation * loudness
    return jnp.minimum(jnp.maximum(result, -most), most).astype(held_as)


def setup_inputs(seed: int = 0) -> dict:
    seeds = jax.random.split(jax.random.key(seed), 10)
    first_half = centred(seeds[0], (TOKENS, D), 1.0, 6.0, ((0, 128),))
    second_half = centred(seeds[1], (TOKENS, D), 1.0, 6.0, ((0, 128),))
    second_grad = centred(seeds[2], (TOKENS, D), 0.5, 3.0, ((0, 128),))
    norm_gain = jnp.clip(1.0 + 0.1 * jax.random.normal(seeds[3], (D,), jnp.float32), 0.5, 1.5).astype(jnp.bfloat16)
    expert_ids_keys = jax.random.split(jax.random.fold_in(seeds[4], 1), TOKENS // TOK_DEV)
    expert_ids_turns = jax.random.permutation(jax.random.fold_in(seeds[4], 3), TOKENS // TOK_DEV)
    expert_ids = jax.vmap(lambda own, number: routed_block(jax.random.fold_in(seeds[4], 2), own, number, TOK_DEV, EXPERTS, TOP, CAP, 2))(expert_ids_keys, expert_ids_turns).reshape((TOKENS, TOP))
    gates = jnp.clip(jnp.exp(math.log(0.3) - 2.7080503 * jax.random.uniform(seeds[5], (TOKENS, TOP), jnp.float32) ** shard_levels(seeds[5], (TOKENS, TOP), ((0, 128),), -0.2, 0.2)), 0.02, 0.3)
    w_gate = centred(seeds[6], (EXPERTS, D, FF), D ** -0.5, 0.125, ((0, 128), (2, 2)))
    w_up = centred(seeds[7], (EXPERTS, D, FF), D ** -0.5, 0.125, ((0, 128), (2, 2)))
    w_down = centred(seeds[8], (EXPERTS, FF, D), FF ** -0.5, 0.21875, ((0, 128), (1, 2)))
    return {"first_half": first_half, "second_half": second_half, "second_grad": second_grad, "norm_gain": norm_gain, "expert_ids": expert_ids, "gates": gates, "w_gate": w_gate, "w_up": w_up, "w_down": w_down}


EPSILON = 1e-06

def contract_rows(left, right):
    return lax.dot_general(left, right, (((0,), (0,)), ((), ())), preferred_element_type=jnp.float32)

def contract_cols(left, right):
    return lax.dot_general(left, right, (((1,), (1,)), ((), ())), preferred_element_type=jnp.float32)

def expert_pass(row_inputs, row_scaled, gate_mat, up_mat, down_mat):
    gate_pre = jnp.dot(row_inputs, gate_mat, preferred_element_type=jnp.float32)
    up_pre = jnp.dot(row_inputs, up_mat, preferred_element_type=jnp.float32)
    sigmoid_gate = jax.nn.sigmoid(gate_pre)
    swish_gate = gate_pre * sigmoid_gate
    hidden = (swish_gate * up_pre).astype(jnp.bfloat16)
    output = jnp.dot(hidden, down_mat, preferred_element_type=jnp.float32)
    hidden_grad = contract_cols(row_scaled, down_mat)
    gate_grad = (hidden_grad * up_pre * sigmoid_gate * (1.0 + gate_pre * (1.0 - sigmoid_gate))).astype(jnp.bfloat16)
    up_grad = (hidden_grad * swish_gate).astype(jnp.bfloat16)
    input_grad = contract_cols(gate_grad, gate_mat) + contract_cols(up_grad, up_mat)
    return (output, input_grad, contract_rows(hidden, row_scaled))

def reference(first_half, second_half, second_grad, norm_gain, expert_ids, gates, w_gate, w_up, w_down):
    tokens_all, model_width = first_half.shape
    top_count = expert_ids.shape[1]
    experts_all = w_gate.shape[0]
    assigned = tokens_all * top_count
    sources = tokens_all // TOK_DEV
    flat_ids = expert_ids.reshape(assigned).astype(jnp.int32)
    block_of = (jnp.arange(assigned, dtype=jnp.int32) // (TOK_DEV * top_count)).astype(jnp.int32)
    sort_keys = block_of * experts_all + flat_ids
    sort_order = jnp.argsort(sort_keys, stable=True).astype(jnp.int32)
    sorted_keys = sort_keys[sort_order]
    first_pos = jnp.searchsorted(sorted_keys, sorted_keys, side='left').astype(jnp.int32)
    rank_in_block = jnp.zeros((assigned,), jnp.int32).at[sort_order].set(jnp.arange(assigned, dtype=jnp.int32) - first_pos)
    per_expert = sources * CAP
    position = flat_ids * per_expert + block_of * CAP + rank_in_block
    slot_table = jnp.full((experts_all * per_expert,), assigned, jnp.int32).at[position].set(jnp.arange(assigned, dtype=jnp.int32))
    slot_table = slot_table.reshape(experts_all, per_expert)
    values = first_half.astype(jnp.float32)
    inverse = lax.rsqrt(lax.optimization_barrier(jnp.mean(values * values, axis=1, keepdims=True)) + EPSILON)
    gain_value = norm_gain.astype(jnp.float32)
    normed = (values * inverse * gain_value).astype(jnp.bfloat16)
    cotangent = second_grad.astype(jnp.float32)
    flat_gates = gates.reshape(assigned)
    zero_half = jnp.zeros((), jnp.bfloat16)

    def per_expert_step(running, inputs):
        sub_total, grad_total, gate_total = running
        index_row, gate_mat, up_mat, down_mat = inputs
        is_live = index_row < assigned
        clamped = jnp.minimum(index_row, assigned - 1)
        token_rows = clamped // top_count
        row_gates = flat_gates[clamped]
        row_inputs = jnp.where(is_live[:, None], normed[token_rows], zero_half)
        row_scaled = jnp.where(is_live[:, None], (row_gates[:, None] * cotangent[token_rows]).astype(jnp.bfloat16), zero_half)
        output, input_grad, grad_down = expert_pass(row_inputs, row_scaled, gate_mat, up_mat, down_mat)
        out_float = lax.optimization_barrier(output.astype(jnp.bfloat16)).astype(jnp.float32)
        grad_float = lax.optimization_barrier(input_grad.astype(jnp.bfloat16)).astype(jnp.float32)
        sub_total = sub_total.at[token_rows].add(jnp.where(is_live[:, None], row_gates[:, None] * out_float, 0.0))
        grad_total = grad_total.at[token_rows].add(jnp.where(is_live[:, None], grad_float, 0.0))
        gate_term = lax.optimization_barrier(jnp.sum(cotangent[token_rows] * out_float, axis=1))
        gate_total = gate_total.at[clamped].add(jnp.where(is_live, gate_term, 0.0))
        return ((sub_total, grad_total, gate_total), grad_down.astype(jnp.bfloat16))
    start = (jnp.zeros((tokens_all, model_width), jnp.float32), jnp.zeros((tokens_all, model_width), jnp.float32), jnp.zeros((assigned,), jnp.float32))
    finals, stacked = lax.scan(per_expert_step, start, (slot_table, w_gate, w_up, w_down))
    sub_total, grad_total, gate_total = finals
    inverted = (second_half.astype(jnp.float32) - sub_total).astype(jnp.bfloat16)
    gates_grad = gate_total.reshape(tokens_all, top_count)
    normed_grad = grad_total * gain_value
    first_grad = (inverse * normed_grad - values * inverse * inverse * inverse * lax.optimization_barrier(jnp.mean(normed_grad * values, axis=1, keepdims=True))).astype(jnp.bfloat16)
    return (inverted, first_grad, gates_grad, stacked)
```

```python
import jax
import jax.numpy as jnp
import numpy as np
from jax import lax
from jax.experimental import pallas as pl
from jax.experimental.pallas import tpu as pltpu
from jax.sharding import PartitionSpec as P

EPSILON = 1e-06
MESH = pl.DeviceIdType.MESH
BF = jnp.bfloat16
F32 = jnp.float32

NX, NZ, NY = 4, 8, 4
PLANE = NX * NY
TOK = 128
WIDTH = 2048
FF = 768
HALF = FF // 2
TOP = 8
SHARE = 5
SEG = NZ * SHARE
ROWS = PLANE * SEG
UNITS = 4
FU = WIDTH // UNITS
HU = FU // 2
PARTS = 2
PROWS, PCHIPS = ROWS // PARTS, PLANE // PARTS
PTOK, PBLK = NZ * TOK // PARTS, NZ // PARTS


def nt(left, right):
    return lax.dot_general(left, right, (((1,), (1,)), ((), ())), preferred_element_type=F32)


def tn(left, right):
    return lax.dot_general(left, right, (((0,), (0,)), ((), ())), preferred_element_type=F32)


def nn(left, right):
    return jnp.dot(left, right, preferred_element_type=F32)


def kernel(
    first_ref, second_ref, cot_ref, gain_ref, ids_ref, gates_ref, owner_ref, rank_ref,
    wg_hbm, wu_hbm, wd_hbm,
    inv_ref, fg_ref, gg_ref, wdg_hbm,
    wg, wu, wd, ag, meta, sel, selt, gslot, sgsel, sbuf, drecv, rrecv, acc, hid, ggr, ugr,
    rsrecv, wsend, wrecv, dots, dbuf, drx, ggx, obuf, orecv,
    wl_sem, wss, wrs, ags, agr, sbs, sbr, ms, mr, dss, dsr, rss, rsr, ts, tr, qs, qr,
    wgs, wgr, ds_, dr_, es, er, wos, free,
):
    r = lax.axis_index("rep")
    ep = lax.axis_index("ep")
    x, z, y = ep // (NZ * NY), (ep // NY) % NZ, ep % NY

    def at(dx, dz, dy):
        return {"ep": (((x + dx) % NX) * NZ + (z + dz) % NZ) * NY + (y + dy) % NY}

    sib = {"rep": 1 - r}

    def rc(src, dst, send, recv, dev):
        return pltpu.make_async_remote_copy(
            src_ref=src, dst_ref=dst, send_sem=send, recv_sem=recv,
            device_id=dev, device_id_type=MESH,
        )

    barrier = pltpu.get_barrier_semaphore()
    pl.semaphore_signal(barrier, inc=1, device_id=sib, device_id_type=MESH)

    @pl.loop(1, NZ)
    def _(d):
        pl.semaphore_signal(barrier, inc=1, device_id=at(0, d, 0), device_id_type=MESH)

    @pl.loop(1, PLANE)
    def _(n):
        pl.semaphore_signal(barrier, inc=1, device_id=at(n // NY, 0, n % NY), device_id_type=MESH)

    def local_weights():
        cols = pl.ds(pl.multiple_of(r * HALF, 128), HALF)
        return [
            pltpu.make_async_copy(wg_hbm, wg.at[:, cols], wl_sem.at[0]),
            pltpu.make_async_copy(wu_hbm, wu.at[:, cols], wl_sem.at[1]),
            pltpu.make_async_copy(wd_hbm, wd.at[cols, :], wl_sem.at[2]),
        ]

    def sibling_weights():
        cols = pl.ds(pl.multiple_of(r * HALF, 128), HALF)
        return [
            rc(wg_hbm, wg.at[:, cols], wss.at[0], wrs.at[0], sib),
            rc(wu_hbm, wu.at[:, cols], wss.at[1], wrs.at[1], sib),
            rc(wd_hbm, wd.at[cols, :], wss.at[2], wrs.at[2], sib),
        ]

    for copy in local_weights():
        copy.start()

    values = first_ref[...].astype(F32)
    inverse = lax.rsqrt(jnp.mean(values * values, axis=1, keepdims=True) + EPSILON)
    normed = (values * inverse * gain_ref[...].astype(F32)).astype(BF)
    for u in range(UNITS):
        ag[0, u, 0] = normed[:, u * FU : (u + 1) * FU]
        ag[1, u, 0] = cot_ref[:, u * FU : (u + 1) * FU]
    eye = (
        lax.broadcasted_iota(jnp.int32, (TOK, TOK), 0)
        == lax.broadcasted_iota(jnp.int32, (TOK, TOK), 1)
    ).astype(F32)
    ids_t = lax.dot_general(
        ids_ref[...].astype(F32), eye, (((0,), (0,)), ((), ())),
        preferred_element_type=F32, precision=lax.Precision.HIGHEST,
    )
    meta[0, 0:TOP] = ids_t
    meta[0, TOP : 2 * TOP] = gates_ref[...]

    pl.semaphore_wait(barrier, NZ + PLANE - 1)

    def ag_copy(u, way, step):
        sign = 1 - 2 * way
        src = (NZ - (step - 1)) % NZ if way == 0 else step - 1
        dst = NZ - step if way == 0 else step
        cols = slice(None)
        if step == 4:
            cols = slice(0, HU) if way == 0 else slice(HU, FU)
        return rc(
            ag.at[r, u, src, :, cols], ag.at[r, u, dst, :, cols],
            ags.at[u, way, step - 1], agr.at[u, way, step - 1], at(0, sign, 0),
        )

    def sib_copy(u, j):
        return rc(ag.at[r, u, j], ag.at[r, u, j], sbs.at[u, j], sbr.at[u, j], sib)

    def sib_wait(u, j):
        return rc(ag.at[1 - r, u, j], ag.at[1 - r, u, j], sbs.at[u, j], sbr.at[u, j], sib)

    def ag_first(u):
        ag_copy(u, 0, 1).start()
        ag_copy(u, 1, 1).start()

    def ag_next(u, step):
        for way in range(2):
            ag_copy(u, way, step - 1).wait_recv()
            ag_copy(u, way, step).start()
        for j in (NZ - (step - 1), step - 1):
            sib_copy(u, j).start()

    ag_first(0)

    def meta_copy(d):
        return rc(meta.at[0], meta.at[NZ - d], ms.at[d], mr.at[NZ - d], at(0, d, 0))

    @pl.loop(1, NZ)
    def _(d):
        meta_copy(d).start()

    for copy in sibling_weights():
        copy.start()

    @pl.loop(1, NZ)
    def _(d):
        meta_copy(d).wait_recv()

    d_index = lax.broadcasted_iota(jnp.int32, (PLANE, 1), 0)
    dx, dy = d_index >> 2, d_index & 3
    ex, ey = x + dx, y + dy
    ex = jnp.where(ex >= NX, ex - NX, ex)
    ey = jnp.where(ey >= NY, ey - NY, ey)

    def experts_of(plane):
        return ((ex * NZ + plane) * NY + ey).astype(F32)

    experts = experts_of(z)
    before = (
        lax.broadcasted_iota(jnp.int32, (TOK, TOK), 0)
        < lax.broadcasted_iota(jnp.int32, (TOK, TOK), 1)
    ).astype(BF)
    gslot[...] = jnp.zeros_like(gslot)
    owner = owner_ref[...]
    first_rank = (r * SHARE).astype(F32)
    for j in range(NZ):
        hits = jnp.zeros((PLANE, TOK), F32)
        weight = jnp.zeros((PLANE, TOK), F32)
        for k in range(TOP):
            match = meta[j, k : k + 1, :] == experts
            hits = hits + jnp.where(match, 1.0, 0.0)
            weight = weight + jnp.where(match, meta[j, TOP + k : TOP + k + 1, :], 0.0)
        rank = nn(hits.astype(BF), before)
        rank = jnp.where(hits > 0.0, rank, -1.0)
        slot_rank = nn(owner.astype(BF), rank.astype(BF))
        chosen = jnp.where(slot_rank == rank_ref[:, j : j + 1] + first_rank, 1.0, 0.0)
        slot_gate = jnp.dot(
            owner, weight, preferred_element_type=F32, precision=lax.Precision.HIGHEST
        )
        gslot[...] += jnp.sum(chosen * slot_gate, axis=1, keepdims=True)
        sel[:, j * TOK : (j + 1) * TOK] = chosen.astype(BF)
        selt[j * TOK : (j + 1) * TOK, :] = chosen.T.astype(BF)

    def back(n):
        i, j = n // NY, n % NY
        return ((NX - i) % NX) * NY + (NY - j) % NY

    def disp_copy(u, n):
        m = back(n)
        return rc(sbuf.at[u, n], drecv.at[u, m], dss.at[u, n], dsr.at[u, m], at(n // NY, 0, n % NY))

    def ret_copy(u, n):
        m = back(n)
        return rc(sbuf.at[u, n], rrecv.at[u, m], rss.at[u, n], rsr.at[u, m], at(n // NY, 0, n % NY))

    def select(u):
        @pl.loop(0, PARTS)
        def _(c):
            part = pl.ds(pl.multiple_of(c * PROWS, PROWS), PROWS)
            chips = pl.ds(c * PCHIPS, PCHIPS)
            rows = nn(sel[part, :], ag[0, u].reshape(NZ * TOK, FU)).astype(BF)
            sbuf[u, chips, :, 0:FU] = rows.reshape(PCHIPS, SEG, FU)
            cots = nn(sel[part, :], ag[1, u].reshape(NZ * TOK, FU))
            sgsel[u, part, :] = cots.astype(BF)
            scaled = (cots * gslot[part, :]).astype(BF)
            sbuf[u, chips, :, FU:] = scaled.reshape(PCHIPS, SEG, FU)

        drecv[u, 0] = sbuf[u, 0]

        @pl.loop(1, PLANE)
        def _(n):
            disp_copy(u, n).start()

    @pl.loop(0, UNITS + 1)
    def _(p):
        u = p - 1

        @pl.when((p >= 1) & (p < UNITS))
        def _():
            ag_first(p)

        @pl.when(p >= 1)
        def _():
            ag_next(u, 3)

        @pl.when(p < UNITS)
        def _():
            ag_next(p, 2)

        @pl.when(p >= 1)
        def _():
            ag_next(u, 4)
            ag_copy(u, 0, 4).wait_recv()
            ag_copy(u, 1, 4).wait_recv()
            sib_copy(u, 4).start()
            for j in range(1, NZ):
                sib_wait(u, j).wait_recv()
            select(u)

    @pl.loop(0, UNITS)
    def _(u):
        for step in range(1, 5):
            ag_copy(u, 0, step).wait_send()
            ag_copy(u, 1, step).wait_send()
        for j in range(1, NZ):
            sib_copy(u, j).wait_send()

    pl.semaphore_signal(free, inc=1, device_id=sib, device_id_type=MESH)

    for copy in local_weights():
        copy.wait()
    for copy in sibling_weights():
        copy.wait_send()
    other = pl.ds(pl.multiple_of((1 - r) * HALF, 128), HALF)
    rc(wg_hbm, wg.at[:, other], wss.at[0], wrs.at[0], sib).wait_recv()
    rc(wu_hbm, wu.at[:, other], wss.at[1], wrs.at[1], sib).wait_recv()
    rc(wd_hbm, wd.at[other, :], wss.at[2], wrs.at[2], sib).wait_recv()

    acc[...] = jnp.zeros_like(acc)

    @pl.loop(0, UNITS)
    def _(u):
        @pl.loop(1, PLANE)
        def _(n):
            disp_copy(u, n).wait_recv()

        feats = pl.ds(pl.multiple_of(u * FU, FU), FU)

        @pl.loop(0, PARTS)
        def _(c):
            part = pl.ds(pl.multiple_of(c * PROWS, PROWS), PROWS)
            chips = pl.ds(c * PCHIPS, PCHIPS)
            rows = drecv[u, chips, :, 0:FU].reshape(PROWS, FU)
            acc[0, part, :] += nn(rows, wg[feats, :])
            acc[1, part, :] += nn(rows, wu[feats, :])
            cots = drecv[u, chips, :, FU:].reshape(PROWS, FU)
            acc[2, part, :] += nt(cots, wd[:, feats])

    @pl.loop(0, ROWS // 80)
    def _(c):
        part = pl.ds(pl.multiple_of(c * 80, 16), 80)
        gate_pre, up_pre, grad = acc[0, part, :], acc[1, part, :], acc[2, part, :]
        sig = jax.nn.sigmoid(gate_pre)
        swish = gate_pre * sig
        hid[part, :] = (swish * up_pre).astype(BF)
        ggr[part, :] = (grad * up_pre * sig * (1.0 + gate_pre * (1.0 - sig))).astype(BF)
        ugr[part, :] = (grad * swish).astype(BF)

    @pl.loop(0, UNITS)
    def _(u):
        @pl.loop(1, PLANE)
        def _(n):
            disp_copy(u, n).wait_send()

        feats = pl.ds(pl.multiple_of(u * FU, FU), FU)

        @pl.loop(0, PARTS)
        def _(c):
            part = pl.ds(pl.multiple_of(c * PROWS, PROWS), PROWS)
            chips = pl.ds(c * PCHIPS, PCHIPS)
            outs = nn(hid[part, :], wd[:, feats]).astype(BF)
            sbuf[u, chips, :, 0:FU] = outs.reshape(PCHIPS, SEG, FU)
            grads = (nt(ggr[part, :], wg[feats, :]) + nt(ugr[part, :], wu[feats, :])).astype(BF)
            sbuf[u, chips, :, FU:] = grads.reshape(PCHIPS, SEG, FU)

        rrecv[u, 0] = sbuf[u, 0]

        @pl.loop(1, PLANE)
        def _(n):
            ret_copy(u, n).start()

    def wd_copy(u):
        return rc(wsend.at[u], wrecv.at[u], wgs.at[u], wgr.at[u], sib)

    @pl.loop(0, UNITS)
    def _(u):
        half = hid[:, pl.ds(pl.multiple_of((1 - r) * HALF, 128), HALF)]
        wsend[u] = tn(half, drecv[u, :, :, FU:].reshape(ROWS, FU)).astype(BF)
        wd_copy(u).start()

    def wd_out(u):
        feats = pl.ds(pl.multiple_of(u * FU, FU), FU)
        return pltpu.make_async_copy(wsend.at[u], wdg_hbm.at[:, feats], wos.at[u])

    mine = pl.ds(pl.multiple_of(r * HALF, 128), HALF)

    @pl.loop(0, UNITS)
    def _(u):
        feats = pl.ds(pl.multiple_of(u * FU, FU), FU)
        part = tn(hid[:, mine], drecv[u, :, :, FU:].reshape(ROWS, FU))
        rc(wsend.at[u], wrecv.at[u], wgs.at[u], wgr.at[u], sib).wait_recv()
        wd_copy(u).wait_send()
        wsend[u] = (part + wrecv[u].astype(F32)).astype(BF)
        wd_out(u).start()

    def t_copy(u):
        return rc(ag.at[0, u], ag.at[1, u], ts.at[u], tr.at[u], sib)

    dots[...] = jnp.zeros_like(dots)
    pl.semaphore_wait(free, 1)

    def combine_other(u):
        @pl.loop(1, PLANE)
        def _(n):
            ret_copy(u, n).wait_recv()

        @pl.loop(0, PARTS)
        def _(c):
            part = pl.ds(pl.multiple_of(c * PROWS, PROWS), PROWS)
            chips = pl.ds(c * PCHIPS, PCHIPS)
            outs = rrecv[u, chips, :, 0:FU].astype(F32).reshape(PROWS, FU)
            dots[part, :] += jnp.sum(outs * sgsel[u, part, :].astype(F32), axis=1, keepdims=True)
            rrecv[u, chips, :, 0:FU] = (outs * gslot[part, :]).astype(BF).reshape(PCHIPS, SEG, FU)

        kept = rrecv[u, :, :, pl.ds(pl.multiple_of((1 - r) * FU, FU), FU)].reshape(ROWS, FU)

        @pl.loop(0, PARTS)
        def _(c):
            part = pl.ds(pl.multiple_of(c * PTOK, PTOK), PTOK)
            blocks = pl.ds(c * PBLK, PBLK)
            ag[0, u, blocks] = nn(selt[part, :], kept).astype(BF).reshape(PBLK, TOK, FU)

        t_copy(u).start()

    def combine_mine(u):
        t_copy(u).wait_recv()
        kept = rrecv[u, :, :, pl.ds(pl.multiple_of(r * FU, FU), FU)].reshape(ROWS, FU)

        @pl.loop(0, PARTS)
        def _(c):
            part = pl.ds(pl.multiple_of(c * PTOK, PTOK), PTOK)
            blocks = pl.ds(c * PBLK, PBLK)
            total = nn(selt[part, :], kept).reshape(PBLK, TOK, FU) + ag[1, u, blocks].astype(F32)
            ag[1, u, blocks] = total.astype(BF)

    def rs_copy(u, way, step):
        sign = 1 - 2 * way
        src = 5 - step if way == 0 else step + 3
        cols = slice(None)
        if step == 1:
            cols = slice(0, HU) if way == 0 else slice(HU, FU)
        return rc(
            ag.at[1, u, src, :, cols], rsrecv.at[u, way, step - 1, :, cols],
            qs.at[u, way, step - 1], qr.at[u, way, step - 1], at(0, sign, 0),
        )

    def rs_next(u, step):
        for way in range(2):
            rs_copy(u, way, step - 1).wait_recv()
            src = 5 - step if way == 0 else step + 3
            cols = slice(0, FU)
            if step == 2:
                cols = slice(0, HU) if way == 0 else slice(HU, FU)
            ag[1, u, src, :, cols] = (
                ag[1, u, src, :, cols].astype(F32)
                + rsrecv[u, way, step - 2, :, cols].astype(F32)
            ).astype(BF)
            rs_copy(u, way, step).start()

    def dots_copy(d):
        return rc(dbuf.at[d], drx.at[NZ - d], ds_.at[d], dr_.at[NZ - d], at(0, d, 0))

    @pl.loop(0, UNITS + 3)
    def _(p):
        @pl.when(p < UNITS)
        def _():
            combine_other(p)

        @pl.when((p >= 1) & (p < UNITS + 1))
        def _():
            u = p - 1
            combine_mine(u)
            rs_copy(u, 0, 1).start()
            rs_copy(u, 1, 1).start()

        @pl.when((p >= 2) & (p < UNITS + 2))
        def _():
            rs_next(p - 2, 3)

        @pl.when((p >= 1) & (p < UNITS + 1))
        def _():
            rs_next(p - 1, 2)

        @pl.when((p >= 2) & (p < UNITS + 2))
        def _():
            rs_next(p - 2, 4)

        @pl.when(p >= 3)
        def _():
            u = p - 3
            rs_copy(u, 0, 4).wait_recv()
            rs_copy(u, 1, 4).wait_recv()
            acc[0, pl.ds(pl.multiple_of(u * TOK, TOK), TOK), 0:FU] = (
                ag[1, u, 0].astype(F32)
                + rsrecv[u, 0, 3].astype(F32)
                + rsrecv[u, 1, 3].astype(F32)
            )

        @pl.when(p == UNITS - 1)
        def _():
            by_owner = owner_ref[...] * dots[...]
            for j in range(NZ):
                dbuf[j] = lax.dot_general(
                    by_owner, sel[:, j * TOK : (j + 1) * TOK].astype(F32),
                    (((0,), (0,)), ((), ())),
                    preferred_element_type=F32, precision=lax.Precision.HIGHEST,
                )

            @pl.loop(1, NZ)
            def _(d):
                dots_copy(d).start()

    drx[0] = dbuf[0]

    @pl.loop(1, NZ)
    def _(d):
        dots_copy(d).wait_recv()

    ids_t = meta[0, 0:TOP]
    rows = []
    for k in range(TOP):
        got = jnp.zeros((PLANE, TOK), F32)
        for m in range(NZ):
            plane = z + m
            plane = jnp.where(plane >= NZ, plane - NZ, plane)
            got = got + jnp.where(ids_t[k : k + 1, :] == experts_of(plane), drx[m], 0.0)
        rows.append(jnp.sum(got, axis=0, keepdims=True))
    ggx[0] = jnp.concatenate(rows, axis=0)
    gg_copy = rc(ggx.at[0], ggx.at[1], es.at[0], er.at[0], sib)
    gg_copy.start()

    values = first_ref[...].astype(F32)
    inverse = lax.rsqrt(jnp.mean(values * values, axis=1, keepdims=True) + EPSILON)
    total = jnp.concatenate([acc[0, u * TOK : (u + 1) * TOK, 0:FU] for u in range(UNITS)], axis=1)

    @pl.when(r == 0)
    def _():
        obuf[...] = (second_ref[...].astype(F32) - total).astype(BF)

    @pl.when(r == 1)
    def _():
        grad = total * gain_ref[...].astype(F32)
        obuf[...] = (
            inverse * grad
            - values * inverse * inverse * inverse * jnp.mean(grad * values, axis=1, keepdims=True)
        ).astype(BF)

    out_copy = rc(obuf, orecv, es.at[1], er.at[1], sib)
    out_copy.start()

    @pl.loop(0, UNITS)
    def _(u):
        @pl.loop(1, PLANE)
        def _(n):
            ret_copy(u, n).wait_send()

        for step in range(1, 5):
            rs_copy(u, 0, step).wait_send()
            rs_copy(u, 1, step).wait_send()
        t_copy(u).wait_send()
        wd_out(u).wait()

    @pl.loop(1, NZ)
    def _(d):
        dots_copy(d).wait_send()
        meta_copy(d).wait_send()

    gg_copy.wait()
    gg_ref[...] = ggx[0] + ggx[1]
    out_copy.wait()

    @pl.when(r == 0)
    def _():
        inv_ref[...] = obuf[...]
        fg_ref[...] = orecv[...]

    @pl.when(r == 1)
    def _():
        inv_ref[...] = orecv[...]
        fg_ref[...] = obuf[...]


def slot_tables():
    slot = np.arange(ROWS)
    owner = (slot[:, None] // SEG == np.arange(PLANE)[None, :]).astype(np.float32)
    block, order = slot % SEG // SHARE, slot % SHARE
    rank = np.where(block[:, None] == np.arange(NZ)[None, :], order[:, None], -100)
    return owner, rank.astype(np.float32)


def local(first, second, cot, gain, ids, gates, w_gate, w_up, w_down):
    owner, rank = slot_tables()
    vmem = pl.BlockSpec(memory_space=pltpu.VMEM)
    hbm = pl.BlockSpec(memory_space=pl.ANY)
    dma = pltpu.SemaphoreType.DMA
    inv, fg, gg, wdg = pl.pallas_call(
        kernel,
        out_shape=(
            jax.ShapeDtypeStruct((TOK, WIDTH), BF),
            jax.ShapeDtypeStruct((TOK, WIDTH), BF),
            jax.ShapeDtypeStruct((TOP, TOK), F32),
            jax.ShapeDtypeStruct((HALF, WIDTH), BF),
        ),
        in_specs=[vmem] * 8 + [hbm] * 3,
        out_specs=(vmem, vmem, vmem, hbm),
        scratch_shapes=[
            pltpu.VMEM((WIDTH, FF), BF),
            pltpu.VMEM((WIDTH, FF), BF),
            pltpu.VMEM((FF, WIDTH), BF),
            pltpu.VMEM((2, UNITS, NZ, TOK, FU), BF),
            pltpu.VMEM((NZ, 2 * TOP, TOK), F32),
            pltpu.VMEM((ROWS, NZ * TOK), BF),
            pltpu.VMEM((NZ * TOK, ROWS), BF),
            pltpu.VMEM((ROWS, 1), F32),
            pltpu.VMEM((UNITS, ROWS, FU), BF),
            pltpu.VMEM((UNITS, PLANE, SEG, 2 * FU), BF),
            pltpu.VMEM((UNITS, PLANE, SEG, 2 * FU), BF),
            pltpu.VMEM((UNITS, PLANE, SEG, 2 * FU), BF),
            pltpu.VMEM((3, ROWS, FF), F32),
            pltpu.VMEM((ROWS, FF), BF),
            pltpu.VMEM((ROWS, FF), BF),
            pltpu.VMEM((ROWS, FF), BF),
            pltpu.VMEM((UNITS, 2, 4, TOK, FU), BF),
            pltpu.VMEM((UNITS, HALF, FU), BF),
            pltpu.VMEM((UNITS, HALF, FU), BF),
            pltpu.VMEM((ROWS, 1), F32),
            pltpu.VMEM((NZ, PLANE, TOK), F32),
            pltpu.VMEM((NZ, PLANE, TOK), F32),
            pltpu.VMEM((2, TOP, TOK), F32),
            pltpu.VMEM((TOK, WIDTH), BF),
            pltpu.VMEM((TOK, WIDTH), BF),
            dma((3,)), dma((3,)), dma((3,)),
            dma((UNITS, 2, 4)), dma((UNITS, 2, 4)),
            dma((UNITS, NZ)), dma((UNITS, NZ)),
            dma((NZ,)), dma((NZ,)),
            dma((UNITS, PLANE)), dma((UNITS, PLANE)),
            dma((UNITS, PLANE)), dma((UNITS, PLANE)),
            dma((UNITS,)), dma((UNITS,)),
            dma((UNITS, 2, 4)), dma((UNITS, 2, 4)),
            dma((UNITS,)), dma((UNITS,)),
            dma((NZ,)), dma((NZ,)),
            dma((2,)), dma((2,)), dma((UNITS,)), pltpu.SemaphoreType.REGULAR,
        ],
        compiler_params=pltpu.CompilerParams(
            collective_id=1, has_side_effects=True, vmem_limit_bytes=63 << 20
        ),
        name="experts_backward",
    )(
        first, second, cot, gain.reshape(1, WIDTH), ids, gates.T,
        jnp.asarray(owner), jnp.asarray(rank), w_gate[0], w_up[0], w_down[0],
    )
    return inv, fg, gg.T, wdg[None]


def solution(mesh):
    rows = P("ep", None)
    return jax.shard_map(
        local,
        mesh=mesh,
        in_specs=(
            rows, rows, rows, P(), rows, rows,
            P("ep", None, "rep"), P("ep", None, "rep"), P("ep", "rep", None),
        ),
        out_specs=(rows, rows, rows, P("ep", "rep", None)),
        check_vma=False,
    )
```

```python
import jax
import jax.numpy as jnp
import numpy as np
from jax import lax
from jax.experimental import pallas as pl
from jax.experimental.pallas import tpu as pltpu
from jax.sharding import PartitionSpec as P

EPSILON = 1e-06
MESH = pl.DeviceIdType.MESH
BF = jnp.bfloat16
F32 = jnp.float32

NX, NZ, NY = 4, 8, 4
PLANE = NX * NY
TOK = 128
WIDTH = 2048
FF = 768
HALF = FF // 2
TOP = 8
SHARE = 5
SEG = NZ * SHARE
ROWS = PLANE * SEG
UNITS = 8
FU = WIDTH // UNITS
HU = FU // 2
PARTS = 2
PROWS, PCHIPS = ROWS // PARTS, PLANE // PARTS
AHEAD = 3
ORDER = (10, 6, 14, 9, 11, 5, 7, 13, 15, 2, 8, 1, 4, 3, 12)
LAG = 3
PTOK, PBLK = NZ * TOK // PARTS, NZ // PARTS


def nt(left, right):
    return lax.dot_general(left, right, (((1,), (1,)), ((), ())), preferred_element_type=F32)


def tn(left, right):
    return lax.dot_general(left, right, (((0,), (0,)), ((), ())), preferred_element_type=F32)


def nn(left, right):
    return jnp.dot(left, right, preferred_element_type=F32)


def kernel(
    first_ref, cot_ref, gain_ref, ids_ref, gates_ref, owner_ref, rank_ref,
    wg_hbm, wu_hbm, wd_hbm,
    tot_hbm, gg_ref, wdg_hbm,
    wg, wu, wd, ag, meta, sel, selt, gslot, sgsel, sbuf, drecv, rrecv, acc, hid, ggr, ugr,
    rsrecv, wsend, wrecv, dots, dbuf, drx, ggx,
    wl_sem, wss, wrs, ags, agr, sbs, sbr, ms, mr, dss, dsr, rss, rsr, ts, tr, qs, qr,
    wgs, wgr, ds_, dr_, es, er, wos, tl, tss, trs, free,
):
    r = lax.axis_index("rep")
    ep = lax.axis_index("ep")
    x, z, y = ep // (NZ * NY), (ep // NY) % NZ, ep % NY

    def at(dx, dz, dy):
        return {"ep": (((x + dx) % NX) * NZ + (z + dz) % NZ) * NY + (y + dy) % NY}

    sib = {"rep": 1 - r}

    def rc(src, dst, send, recv, dev):
        return pltpu.make_async_remote_copy(
            src_ref=src, dst_ref=dst, send_sem=send, recv_sem=recv,
            device_id=dev, device_id_type=MESH,
        )

    barrier = pltpu.get_barrier_semaphore()
    pl.semaphore_signal(barrier, inc=1, device_id=sib, device_id_type=MESH)

    @pl.loop(1, NZ)
    def _(d):
        pl.semaphore_signal(barrier, inc=1, device_id=at(0, d, 0), device_id_type=MESH)

    @pl.loop(1, PLANE)
    def _(n):
        pl.semaphore_signal(barrier, inc=1, device_id=at(n // NY, 0, n % NY), device_id_type=MESH)

    def local_weights():
        cols = pl.ds(pl.multiple_of(r * HALF, 128), HALF)
        return [
            pltpu.make_async_copy(wg_hbm, wg.at[:, cols], wl_sem.at[0]),
            pltpu.make_async_copy(wu_hbm, wu.at[:, cols], wl_sem.at[1]),
            pltpu.make_async_copy(wd_hbm, wd.at[cols, :], wl_sem.at[2]),
        ]

    def sibling_weights():
        cols = pl.ds(pl.multiple_of(r * HALF, 128), HALF)
        return [
            rc(wg_hbm, wg.at[:, cols], wss.at[0], wrs.at[0], sib),
            rc(wu_hbm, wu.at[:, cols], wss.at[1], wrs.at[1], sib),
            rc(wd_hbm, wd.at[cols, :], wss.at[2], wrs.at[2], sib),
        ]

    for copy in local_weights():
        copy.start()

    values = first_ref[...].astype(F32)
    inverse = lax.rsqrt(jnp.mean(values * values, axis=1, keepdims=True) + EPSILON)
    normed = (values * inverse * gain_ref[...].astype(F32)).astype(BF)
    for u in range(UNITS):
        ag[0, u, 0] = normed[:, u * FU : (u + 1) * FU]
        ag[1, u, 0] = cot_ref[:, u * FU : (u + 1) * FU]
    meta[0, 0:TOP] = ids_ref[...].astype(F32)
    meta[0, TOP : 2 * TOP] = gates_ref[...]

    pl.semaphore_wait(barrier, NZ + PLANE - 1)

    def ag_copy(u, way, step):
        sign = 1 - 2 * way
        src = (NZ - (step - 1)) % NZ if way == 0 else step - 1
        dst = NZ - step if way == 0 else step
        cols = slice(None)
        if step == 4:
            cols = slice(0, HU) if way == 0 else slice(HU, FU)
        return rc(
            ag.at[r, u, src, :, cols], ag.at[r, u, dst, :, cols],
            ags.at[u, way, step - 1], agr.at[u, way, step - 1], at(0, sign, 0),
        )

    def sib_copy(u, j):
        return rc(ag.at[r, u, j], ag.at[r, u, j], sbs.at[u, j], sbr.at[u, j], sib)

    def sib_wait(u, j):
        return rc(ag.at[1 - r, u, j], ag.at[1 - r, u, j], sbs.at[u, j], sbr.at[u, j], sib)

    def ag_first(u):
        ag_copy(u, 0, 1).start()
        ag_copy(u, 1, 1).start()

    def ag_next(u, step):
        for way in range(2):
            ag_copy(u, way, step - 1).wait_recv()
            ag_copy(u, way, step).start()
        for j in (NZ - (step - 1), step - 1):
            sib_copy(u, j).start()

    ag_first(0)
    ag_first(1)

    sibling_weights()[0].start()
    acc[...] = jnp.zeros_like(acc)
    dots[...] = jnp.zeros_like(dots)

    def meta_copy(d):
        return rc(meta.at[0], meta.at[NZ - d], ms.at[d], mr.at[NZ - d], at(0, d, 0))

    @pl.loop(1, NZ)
    def _(d):
        meta_copy(d).start()

    d_index = lax.broadcasted_iota(jnp.int32, (PLANE, 1), 0)
    dx, dy = d_index >> 2, d_index & 3
    ex, ey = x + dx, y + dy
    ex = jnp.where(ex >= NX, ex - NX, ex)
    ey = jnp.where(ey >= NY, ey - NY, ey)

    def experts_of(plane):
        return ((ex * NZ + plane) * NY + ey).astype(F32)

    experts = experts_of(z)
    before = (
        lax.broadcasted_iota(jnp.int32, (TOK, TOK), 0)
        < lax.broadcasted_iota(jnp.int32, (TOK, TOK), 1)
    ).astype(BF)
    gslot[...] = jnp.zeros_like(gslot)
    owner = owner_ref[...]
    first_rank = (r * SHARE).astype(F32)

    def slots_of(j):
        if j:
            meta_copy(NZ - j).wait_recv()
        hits = jnp.zeros((PLANE, TOK), F32)
        weight = jnp.zeros((PLANE, TOK), F32)
        for k in range(TOP):
            match = meta[j, k : k + 1, :] == experts
            hits = hits + jnp.where(match, 1.0, 0.0)
            weight = weight + jnp.where(match, meta[j, TOP + k : TOP + k + 1, :], 0.0)
        rank = nn(hits.astype(BF), before)
        rank = jnp.where(hits > 0.0, rank, -1.0)
        slot_rank = nn(owner.astype(BF), rank.astype(BF))
        chosen = jnp.where(slot_rank == rank_ref[:, j : j + 1] + first_rank, 1.0, 0.0)
        slot_gate = jnp.dot(
            owner, weight, preferred_element_type=F32, precision=lax.Precision.HIGHEST
        )
        gslot[...] += jnp.sum(chosen * slot_gate, axis=1, keepdims=True)
        sel[:, j * TOK : (j + 1) * TOK] = chosen.astype(BF)
        selt[j * TOK : (j + 1) * TOK, :] = chosen.T.astype(BF)

    slots_of(0)
    slots_of(1)
    ag_next(0, 2)
    slots_of(7)
    slots_of(2)
    ag_next(0, 3)
    ag_next(1, 2)
    slots_of(6)
    slots_of(3)
    ag_first(2)
    ag_next(0, 4)
    ag_next(1, 3)
    slots_of(5)
    slots_of(4)

    def back(n):
        i, j = n // NY, n % NY
        return ((NX - i) % NX) * NY + (NY - j) % NY

    def disp_copy(u, n):
        m = back(n)
        return rc(sbuf.at[u, n], drecv.at[u, m], dss.at[u, n], dsr.at[u, m], at(n // NY, 0, n % NY))

    def ret_copy(u, n):
        m = back(n)
        return rc(sbuf.at[u, n], rrecv.at[u, m], rss.at[u, n], rsr.at[u, m], at(n // NY, 0, n % NY))

    def select(u):
        @pl.loop(0, PARTS)
        def _(c):
            part = pl.ds(pl.multiple_of(c * PROWS, PROWS), PROWS)
            chips = pl.ds(c * PCHIPS, PCHIPS)
            rows = nn(sel[part, :], ag[0, u].reshape(NZ * TOK, FU)).astype(BF)
            sbuf[u, chips, :, 0:FU] = rows.reshape(PCHIPS, SEG, FU)
            cots = nn(sel[part, :], ag[1, u].reshape(NZ * TOK, FU))
            sgsel[u, part, :] = cots.astype(BF)
            scaled = (cots * gslot[part, :]).astype(BF)
            sbuf[u, chips, :, FU:] = scaled.reshape(PCHIPS, SEG, FU)

        drecv[u, 0] = sbuf[u, 0]

        for n in ORDER:
            disp_copy(u, n).start()

    def wait_weights():
        for copy in local_weights():
            copy.wait()
        for copy in sibling_weights():
            copy.wait_send()
        other = pl.ds(pl.multiple_of((1 - r) * HALF, 128), HALF)
        rc(wg_hbm, wg.at[:, other], wss.at[0], wrs.at[0], sib).wait_recv()
        rc(wu_hbm, wu.at[:, other], wss.at[1], wrs.at[1], sib).wait_recv()
        rc(wd_hbm, wd.at[other, :], wss.at[2], wrs.at[2], sib).wait_recv()

    def gather_rows(u):
        @pl.loop(1, PLANE)
        def _(n):
            disp_copy(u, n).wait_recv()

    def project(u, c):
        feats = pl.ds(pl.multiple_of(u * FU, FU), FU)
        part = pl.ds(pl.multiple_of(c * PROWS, PROWS), PROWS)
        chips = pl.ds(c * PCHIPS, PCHIPS)
        rows = drecv[u, chips, :, 0:FU].reshape(PROWS, FU)
        acc[0, part, :] += nn(rows, wg[feats, :])
        acc[1, part, :] += nn(rows, wu[feats, :])
        cots = drecv[u, chips, :, FU:].reshape(PROWS, FU)
        acc[2, part, :] += nt(cots, wd[:, feats])

    def project_all(u):
        gather_rows(u)

        @pl.loop(0, PARTS)
        def _(c):
            project(u, c)

    def activate(c):
        @pl.loop(0, PROWS // 80)
        def _(k):
            part = pl.ds(pl.multiple_of(c * PROWS + k * 80, 16), 80)
            gate_pre, up_pre, grad = acc[0, part, :], acc[1, part, :], acc[2, part, :]
            sig = jax.nn.sigmoid(gate_pre)
            swish = gate_pre * sig
            hid[part, :] = (swish * up_pre).astype(BF)
            ggr[part, :] = (grad * up_pre * sig * (1.0 + gate_pre * (1.0 - sig))).astype(BF)
            ugr[part, :] = (grad * swish).astype(BF)

    def answer(u, c):
        feats = pl.ds(pl.multiple_of(u * FU, FU), FU)
        part = pl.ds(pl.multiple_of(c * PROWS, PROWS), PROWS)
        chips = pl.ds(c * PCHIPS, PCHIPS)
        outs = nn(hid[part, :], wd[:, feats]).astype(BF)
        sbuf[u, chips, :, 0:FU] = outs.reshape(PCHIPS, SEG, FU)
        grads = (nt(ggr[part, :], wg[feats, :]) + nt(ugr[part, :], wu[feats, :])).astype(BF)
        sbuf[u, chips, :, FU:] = grads.reshape(PCHIPS, SEG, FU)

        @pl.loop(0, PCHIPS)
        def _(k):
            n = (c + 1) * PCHIPS - 1 - k

            @pl.when(n > 0)
            def _():
                ret_copy(u, n).start()

    def answer_all(u):
        @pl.loop(0, PARTS)
        def _(c):
            answer(u, c)

        rrecv[u, 0] = sbuf[u, 0]

    @pl.loop(0, UNITS)
    def _(u):
        @pl.when(u + 1 < UNITS)
        def _():
            ag_next(u + 1, 4)

        ag_copy(u, 0, 4).wait_recv()
        ag_copy(u, 1, 4).wait_recv()
        sib_copy(u, 4).start()

        @pl.when(u + 2 < UNITS)
        def _():
            ag_next(u + 2, 2)

        for j in range(1, NZ):
            sib_wait(u, j).wait_recv()
        select(u)

        @pl.when(u + 2 < UNITS)
        def _():
            ag_next(u + 2, 3)

        @pl.when(u + 3 < UNITS)
        def _():
            ag_first(u + 3)

        @pl.when(u == 0)
        def _():
            sibling_weights()[1].start()

        @pl.when(u == 1)
        def _():
            sibling_weights()[2].start()

        @pl.when(u == LAG)
        def _():
            wait_weights()

        @pl.when(u >= LAG)
        def _():
            project_all(u - LAG)

    @pl.loop(0, UNITS)
    def _(u):
        for step in range(1, 5):
            ag_copy(u, 0, step).wait_send()
            ag_copy(u, 1, step).wait_send()
        for j in range(1, NZ):
            sib_copy(u, j).wait_send()

    pl.semaphore_signal(free, inc=1, device_id=sib, device_id_type=MESH)

    @pl.loop(UNITS - LAG, UNITS - 1)
    def _(u):
        project_all(u)

    @pl.loop(0, UNITS)
    def _(u):
        @pl.loop(1, PLANE)
        def _(n):
            disp_copy(u, n).wait_send()

    gather_rows(UNITS - 1)

    @pl.loop(0, PARTS)
    def _(c):
        project(UNITS - 1, c)
        activate(c)
        answer(0, c)

    rrecv[0, 0] = sbuf[0, 0]

    @pl.loop(1, AHEAD)
    def _(u):
        answer_all(u)

    def wd_copy(u):
        return rc(wsend.at[u], wrecv.at[u], wgs.at[u], wgr.at[u], sib)

    def wd_other(u):
        half = hid[:, pl.ds(pl.multiple_of((1 - r) * HALF, 128), HALF)]
        wsend[u] = tn(half, drecv[u, :, :, FU:].reshape(ROWS, FU)).astype(BF)
        wd_copy(u).start()

    def wd_out(u):
        feats = pl.ds(pl.multiple_of(u * FU, FU), FU)
        return pltpu.make_async_copy(wsend.at[u], wdg_hbm.at[:, feats], wos.at[u])

    def wd_mine(u):
        half = hid[:, pl.ds(pl.multiple_of(r * HALF, 128), HALF)]
        part = tn(half, drecv[u, :, :, FU:].reshape(ROWS, FU))
        wd_copy(u).wait_recv()
        wd_copy(u).wait_send()
        wsend[u] = (part + wrecv[u].astype(F32)).astype(BF)
        wd_out(u).start()

    def t_copy(u):
        return rc(ag.at[0, u], ag.at[1, u], ts.at[u], tr.at[u], sib)

    pl.semaphore_wait(free, 1)

    def combine_other(u):
        @pl.loop(1, PLANE)
        def _(n):
            ret_copy(u, n).wait_recv()

        @pl.loop(0, PARTS)
        def _(c):
            part = pl.ds(pl.multiple_of(c * PROWS, PROWS), PROWS)
            chips = pl.ds(c * PCHIPS, PCHIPS)
            outs = rrecv[u, chips, :, 0:FU].astype(F32).reshape(PROWS, FU)
            dots[part, :] += jnp.sum(outs * sgsel[u, part, :].astype(F32), axis=1, keepdims=True)
            rrecv[u, chips, :, 0:FU] = (outs * gslot[part, :]).astype(BF).reshape(PCHIPS, SEG, FU)

        kept = rrecv[u, :, :, pl.ds(pl.multiple_of((1 - r) * FU, FU), FU)].reshape(ROWS, FU)

        @pl.loop(0, PARTS)
        def _(c):
            part = pl.ds(pl.multiple_of(c * PTOK, PTOK), PTOK)
            blocks = pl.ds(c * PBLK, PBLK)
            ag[0, u, blocks] = nn(selt[part, :], kept).astype(BF).reshape(PBLK, TOK, FU)

        t_copy(u).start()

    def combine_mine(u):
        t_copy(u).wait_recv()
        kept = rrecv[u, :, :, pl.ds(pl.multiple_of(r * FU, FU), FU)].reshape(ROWS, FU)

        @pl.loop(0, PARTS)
        def _(c):
            part = pl.ds(pl.multiple_of(c * PTOK, PTOK), PTOK)
            blocks = pl.ds(c * PBLK, PBLK)
            total = nn(selt[part, :], kept).reshape(PBLK, TOK, FU) + ag[1, u, blocks].astype(F32)
            ag[1, u, blocks] = total.astype(BF)

    def rs_copy(u, way, step):
        sign = 1 - 2 * way
        src = 5 - step if way == 0 else step + 3
        cols = slice(None)
        if step == 1:
            cols = slice(0, HU) if way == 0 else slice(HU, FU)
        return rc(
            ag.at[1, u, src, :, cols], rsrecv.at[u, way, step - 1, :, cols],
            qs.at[u, way, step - 1], qr.at[u, way, step - 1], at(0, sign, 0),
        )

    def rs_next(u, step):
        for way in range(2):
            rs_copy(u, way, step - 1).wait_recv()
            src = 5 - step if way == 0 else step + 3
            cols = slice(0, FU)
            if step == 2:
                cols = slice(0, HU) if way == 0 else slice(HU, FU)
            ag[1, u, src, :, cols] = (
                ag[1, u, src, :, cols].astype(F32)
                + rsrecv[u, way, step - 2, :, cols].astype(F32)
            ).astype(BF)
            rs_copy(u, way, step).start()

    def dots_copy(d):
        return rc(dbuf.at[d], drx.at[NZ - d], ds_.at[d], dr_.at[NZ - d], at(0, d, 0))

    def tot_part(u):
        return acc.at[u % 2, pl.ds(pl.multiple_of(u // 2 * TOK, TOK), TOK), 0:FU]

    def tot_copy(u):
        return pltpu.make_async_copy(tot_part(u), tot_hbm.at[r, u], tl.at[u])

    def tot_send(u):
        return rc(tot_part(u), tot_hbm.at[r, u], tss.at[u], trs.at[u], sib)

    def tot_wait(u):
        return rc(tot_part(u), tot_hbm.at[1 - r, u], tss.at[u], trs.at[u], sib)

    gg_copy = rc(ggx.at[0], ggx.at[1], es.at[0], er.at[0], sib)

    @pl.loop(0, UNITS + 5)
    def _(p):
        @pl.when(p >= 5)
        def _():
            u = p - 5
            rs_copy(u, 0, 4).wait_recv()
            rs_copy(u, 1, 4).wait_recv()
            acc[u % 2, pl.ds(pl.multiple_of(u // 2 * TOK, TOK), TOK), 0:FU] = (
                ag[1, u, 0].astype(F32)
                + rsrecv[u, 0, 3].astype(F32)
                + rsrecv[u, 1, 3].astype(F32)
            )
            tot_copy(u).start()
            tot_send(u).start()

        for step in (4, 3, 2):
            @pl.when((p >= step) & (p < UNITS + step))
            def _(step=step):
                rs_next(p - step, step)

        @pl.when((p >= 1) & (p < UNITS + 1))
        def _():
            u = p - 1
            combine_mine(u)
            rs_copy(u, 0, 1).start()
            rs_copy(u, 1, 1).start()

        @pl.when(p + AHEAD < UNITS)
        def _():
            answer_all(p + AHEAD)

        @pl.when(p < UNITS)
        def _():
            wd_other(p)

        @pl.when((p >= 1) & (p < UNITS + 1))
        def _():
            wd_mine(p - 1)

        @pl.when(p < UNITS)
        def _():
            combine_other(p)

        @pl.when(p == UNITS - 1)
        def _():
            by_owner = owner_ref[...] * dots[...]
            for j in range(NZ):
                dbuf[j] = lax.dot_general(
                    by_owner, sel[:, j * TOK : (j + 1) * TOK].astype(F32),
                    (((0,), (0,)), ((), ())),
                    preferred_element_type=F32, precision=lax.Precision.HIGHEST,
                )

            @pl.loop(1, NZ)
            def _(d):
                dots_copy(d).start()

        @pl.when(p == UNITS + 2)
        def _():
            drx[0] = dbuf[0]

            @pl.loop(1, NZ)
            def _(d):
                dots_copy(d).wait_recv()

            ids_t = meta[0, 0:TOP]
            rows = []
            for k in range(TOP):
                got = jnp.zeros((PLANE, TOK), F32)
                for m in range(NZ):
                    plane = z + m
                    plane = jnp.where(plane >= NZ, plane - NZ, plane)
                    got = got + jnp.where(ids_t[k : k + 1, :] == experts_of(plane), drx[m], 0.0)
                rows.append(jnp.sum(got, axis=0, keepdims=True))
            ggx[0] = jnp.concatenate(rows, axis=0)
            gg_copy.start()

    @pl.loop(0, UNITS)
    def _(u):
        @pl.loop(1, PLANE)
        def _(n):
            ret_copy(u, n).wait_send()

        for step in range(1, 5):
            rs_copy(u, 0, step).wait_send()
            rs_copy(u, 1, step).wait_send()
        t_copy(u).wait_send()
        wd_out(u).wait()
        tot_copy(u).wait()
        tot_send(u).wait_send()
        tot_wait(u).wait_recv()

    @pl.loop(1, NZ)
    def _(d):
        dots_copy(d).wait_send()
        meta_copy(d).wait_send()

    gg_copy.wait()
    gg_ref[...] = ggx[0] + ggx[1]


def finish(
    tot, first_ref, second_ref, gain_ref, gates_in, wd_in,
    inv_ref, fg_ref, gg_ref, wd_ref, sem,
):
    copy = pltpu.make_async_copy(wd_in, wd_ref, sem)
    copy.start()
    gg_ref[...] = gates_in[...]
    values = first_ref[...].astype(F32)
    inverse = lax.rsqrt(jnp.mean(values * values, axis=1, keepdims=True) + EPSILON)
    gain = gain_ref[...].astype(F32)
    along = jnp.zeros((TOK, 1), F32)
    for u in range(UNITS):
        cols = slice(u * FU, (u + 1) * FU)
        inv_ref[:, cols] = (second_ref[:, cols].astype(F32) - tot[0, u]).astype(BF)
        along = along + jnp.sum(tot[1, u] * gain[:, cols] * values[:, cols], axis=1, keepdims=True)
    shift = inverse * inverse * inverse * (along / WIDTH)
    for u in range(UNITS):
        cols = slice(u * FU, (u + 1) * FU)
        fg_ref[:, cols] = (
            inverse * (tot[1, u] * gain[:, cols]) - values[:, cols] * shift
        ).astype(BF)
    copy.wait()


def slot_tables():
    slot = np.arange(ROWS)
    owner = (slot[:, None] // SEG == np.arange(PLANE)[None, :]).astype(np.float32)
    block, order = slot % SEG // SHARE, slot % SHARE
    rank = np.where(block[:, None] == np.arange(NZ)[None, :], order[:, None], -100)
    return owner, rank.astype(np.float32)


def local(first, second, cot, gain, ids, gates, w_gate, w_up, w_down):
    owner, rank = slot_tables()
    vmem = pl.BlockSpec(memory_space=pltpu.VMEM)
    hbm = pl.BlockSpec(memory_space=pl.ANY)
    dma = pltpu.SemaphoreType.DMA
    gain = gain.reshape(1, WIDTH)
    tot, gg, wdg = pl.pallas_call(
        kernel,
        out_shape=(
            jax.ShapeDtypeStruct((2, UNITS, TOK, FU), F32),
            jax.ShapeDtypeStruct((TOP, TOK), F32),
            jax.ShapeDtypeStruct((HALF, WIDTH), BF),
        ),
        in_specs=[vmem] * 7 + [hbm] * 3,
        out_specs=(hbm, vmem, hbm),
        scratch_shapes=[
            pltpu.VMEM((WIDTH, FF), BF),
            pltpu.VMEM((WIDTH, FF), BF),
            pltpu.VMEM((FF, WIDTH), BF),
            pltpu.VMEM((2, UNITS, NZ, TOK, FU), BF),
            pltpu.VMEM((NZ, 2 * TOP, TOK), F32),
            pltpu.VMEM((ROWS, NZ * TOK), BF),
            pltpu.VMEM((NZ * TOK, ROWS), BF),
            pltpu.VMEM((ROWS, 1), F32),
            pltpu.VMEM((UNITS, ROWS, FU), BF),
            pltpu.VMEM((UNITS, PLANE, SEG, 2 * FU), BF),
            pltpu.VMEM((UNITS, PLANE, SEG, 2 * FU), BF),
            pltpu.VMEM((UNITS, PLANE, SEG, 2 * FU), BF),
            pltpu.VMEM((3, ROWS, FF), F32),
            pltpu.VMEM((ROWS, FF), BF),
            pltpu.VMEM((ROWS, FF), BF),
            pltpu.VMEM((ROWS, FF), BF),
            pltpu.VMEM((UNITS, 2, 4, TOK, FU), BF),
            pltpu.VMEM((UNITS, HALF, FU), BF),
            pltpu.VMEM((UNITS, HALF, FU), BF),
            pltpu.VMEM((ROWS, 1), F32),
            pltpu.VMEM((NZ, PLANE, TOK), F32),
            pltpu.VMEM((NZ, PLANE, TOK), F32),
            pltpu.VMEM((2, TOP, TOK), F32),
            dma((3,)), dma((3,)), dma((3,)),
            dma((UNITS, 2, 4)), dma((UNITS, 2, 4)),
            dma((UNITS, NZ)), dma((UNITS, NZ)),
            dma((NZ,)), dma((NZ,)),
            dma((UNITS, PLANE)), dma((UNITS, PLANE)),
            dma((UNITS, PLANE)), dma((UNITS, PLANE)),
            dma((UNITS,)), dma((UNITS,)),
            dma((UNITS, 2, 4)), dma((UNITS, 2, 4)),
            dma((UNITS,)), dma((UNITS,)),
            dma((NZ,)), dma((NZ,)),
            dma((1,)), dma((1,)), dma((UNITS,)),
            dma((UNITS,)), dma((UNITS,)), dma((UNITS,)), pltpu.SemaphoreType.REGULAR,
        ],
        compiler_params=pltpu.CompilerParams(
            collective_id=1, has_side_effects=True, vmem_limit_bytes=63 << 20
        ),
        name="experts_backward",
    )(
        first, cot, gain, ids.T, gates.T,
        jnp.asarray(owner), jnp.asarray(rank), w_gate[0], w_up[0], w_down[0],
    )
    inv, fg, gg, wdg = pl.pallas_call(
        finish,
        out_shape=(
            jax.ShapeDtypeStruct((TOK, WIDTH), BF),
            jax.ShapeDtypeStruct((TOK, WIDTH), BF),
            jax.ShapeDtypeStruct((TOP, TOK), F32),
            jax.ShapeDtypeStruct((HALF, WIDTH), BF),
        ),
        in_specs=[vmem] * 5 + [hbm],
        out_specs=(vmem, vmem, vmem, hbm),
        scratch_shapes=[dma(())],
        compiler_params=pltpu.CompilerParams(vmem_limit_bytes=62 << 20),
        name="streams",
    )(tot, first, second, gain, gg, wdg)
    return inv, fg, gg.T, wdg[None]


def solution(mesh):
    rows = P("ep", None)
    return jax.shard_map(
        local,
        mesh=mesh,
        in_specs=(
            rows, rows, rows, P(), rows, rows,
            P("ep", None, "rep"), P("ep", None, "rep"), P("ep", "rep", None),
        ),
        out_specs=(rows, rows, rows, P("ep", "rep", None)),
        check_vma=False,
    )
```

```python
import jax
import jax.numpy as jnp
import numpy as np
from jax import lax
from jax.experimental import pallas as pl
from jax.experimental.pallas import tpu as pltpu
from jax.sharding import PartitionSpec as P

EPSILON = 1e-06
MESH = pl.DeviceIdType.MESH
BF = jnp.bfloat16
F32 = jnp.float32

NX, NZ, NY = 4, 8, 4
PLANE = NX * NY
TOK = 128
WIDTH = 2048
FF = 768
HALF = FF // 2
TOP = 8
SHARE = 5
SEG = NZ * SHARE
ROWS = PLANE * SEG
UNITS = 8
FU = WIDTH // UNITS
HU = FU // 2
PARTS = 2
PROWS, PCHIPS = ROWS // PARTS, PLANE // PARTS
AHEAD = 3
ORDER = (10, 6, 14, 9, 11, 5, 7, 13, 15, 2, 8, 1, 4, 3, 12)
LAG = 3


def nt(left, right):
    return lax.dot_general(left, right, (((1,), (1,)), ((), ())), preferred_element_type=F32)


def nn(left, right):
    return jnp.dot(left, right, preferred_element_type=F32)


def kernel(
    first_ref, cot_ref, gain_ref, ids_ref, gates_ref, owner_ref, rank_ref,
    wg_hbm, wu_hbm, wd_hbm,
    tot_hbm, gg_ref, wdg_hbm,
    wg, wu, wd, ag, meta, sel, selt, gslot, sgsel, sbuf, drecv, rrecv, acc, hid, hidt, ggr, ugr,
    rsrecv, wsend, wrecv, dots, dbuf, drx, ggx,
    wl_sem, wss, wrs, ags, agr, sbs, sbr, ms, mr, dss, dsr, rss, rsr, ts, tr, qs, qr,
    wgs, wgr, ds_, dr_, es, er, wos, tl, tss, trs, free,
):
    r = lax.axis_index("rep")
    ep = lax.axis_index("ep")
    x, z, y = ep // (NZ * NY), (ep // NY) % NZ, ep % NY

    def at(dx, dz, dy):
        return {"ep": (((x + dx) % NX) * NZ + (z + dz) % NZ) * NY + (y + dy) % NY}

    sib = {"rep": 1 - r}

    def rc(src, dst, send, recv, dev):
        return pltpu.make_async_remote_copy(
            src_ref=src, dst_ref=dst, send_sem=send, recv_sem=recv,
            device_id=dev, device_id_type=MESH,
        )

    barrier = pltpu.get_barrier_semaphore()
    pl.semaphore_signal(barrier, inc=1, device_id=sib, device_id_type=MESH)

    @pl.loop(1, NZ)
    def _(d):
        pl.semaphore_signal(barrier, inc=1, device_id=at(0, d, 0), device_id_type=MESH)

    @pl.loop(1, PLANE)
    def _(n):
        pl.semaphore_signal(barrier, inc=1, device_id=at(n // NY, 0, n % NY), device_id_type=MESH)

    def local_weights():
        cols = pl.ds(pl.multiple_of(r * HALF, 128), HALF)
        return [
            pltpu.make_async_copy(wg_hbm, wg.at[:, cols], wl_sem.at[0]),
            pltpu.make_async_copy(wu_hbm, wu.at[:, cols], wl_sem.at[1]),
            pltpu.make_async_copy(wd_hbm, wd.at[cols, :], wl_sem.at[2]),
        ]

    def sibling_weights():
        cols = pl.ds(pl.multiple_of(r * HALF, 128), HALF)
        return [
            rc(wg_hbm, wg.at[:, cols], wss.at[0], wrs.at[0], sib),
            rc(wu_hbm, wu.at[:, cols], wss.at[1], wrs.at[1], sib),
            rc(wd_hbm, wd.at[cols, :], wss.at[2], wrs.at[2], sib),
        ]

    for copy in local_weights():
        copy.start()

    values = first_ref[...].astype(F32)
    inverse = lax.rsqrt(jnp.mean(values * values, axis=1, keepdims=True) + EPSILON)
    normed = (values * inverse * gain_ref[...].astype(F32)).astype(BF)
    for u in range(UNITS):
        ag[0, u, 0] = normed[:, u * FU : (u + 1) * FU]
        ag[1, u, 0] = cot_ref[:, u * FU : (u + 1) * FU]
    meta[0, 0:TOP] = ids_ref[...].astype(F32)
    meta[0, TOP : 2 * TOP] = gates_ref[...]

    pl.semaphore_wait(barrier, NZ + PLANE - 1)

    def ag_copy(u, way, step):
        sign = 1 - 2 * way
        src = (NZ - (step - 1)) % NZ if way == 0 else step - 1
        dst = NZ - step if way == 0 else step
        cols = slice(None)
        if step == 4:
            cols = slice(0, HU) if way == 0 else slice(HU, FU)
        return rc(
            ag.at[r, u, src, :, cols], ag.at[r, u, dst, :, cols],
            ags.at[u, way, step - 1], agr.at[u, way, step - 1], at(0, sign, 0),
        )

    def sib_copy(u, j):
        return rc(ag.at[r, u, j], ag.at[r, u, j], sbs.at[u, j], sbr.at[u, j], sib)

    def sib_wait(u, j):
        return rc(ag.at[1 - r, u, j], ag.at[1 - r, u, j], sbs.at[u, j], sbr.at[u, j], sib)

    def ag_first(u):
        ag_copy(u, 0, 1).start()
        ag_copy(u, 1, 1).start()

    def ag_next(u, step):
        for way in range(2):
            ag_copy(u, way, step - 1).wait_recv()
            ag_copy(u, way, step).start()
        for j in (NZ - (step - 1), step - 1):
            sib_copy(u, j).start()

    ag_first(0)
    ag_first(1)

    sibling_weights()[0].start()
    acc[...] = jnp.zeros_like(acc)
    dots[...] = jnp.zeros_like(dots)

    def meta_copy(d):
        return rc(meta.at[0], meta.at[NZ - d], ms.at[d], mr.at[NZ - d], at(0, d, 0))

    @pl.loop(1, NZ)
    def _(d):
        meta_copy(d).start()

    d_index = lax.broadcasted_iota(jnp.int32, (PLANE, 1), 0)
    dx, dy = d_index >> 2, d_index & 3
    ex, ey = x + dx, y + dy
    ex = jnp.where(ex >= NX, ex - NX, ex)
    ey = jnp.where(ey >= NY, ey - NY, ey)

    def experts_of(plane):
        return ((ex * NZ + plane) * NY + ey).astype(F32)

    experts = experts_of(z)
    before = (
        lax.broadcasted_iota(jnp.int32, (TOK, TOK), 0)
        < lax.broadcasted_iota(jnp.int32, (TOK, TOK), 1)
    ).astype(BF)
    gslot[...] = jnp.zeros_like(gslot)
    owner = owner_ref[...]
    first_rank = (r * SHARE).astype(F32)

    def slots_of(j):
        if j:
            meta_copy(NZ - j).wait_recv()
        hits = jnp.zeros((PLANE, TOK), F32)
        weight = jnp.zeros((PLANE, TOK), F32)
        for k in range(TOP):
            match = meta[j, k : k + 1, :] == experts
            hits = hits + jnp.where(match, 1.0, 0.0)
            weight = weight + jnp.where(match, meta[j, TOP + k : TOP + k + 1, :], 0.0)
        rank = nn(hits.astype(BF), before)
        rank = jnp.where(hits > 0.0, rank, -1.0)
        slot_rank = nn(owner.astype(BF), rank.astype(BF))
        chosen = jnp.where(slot_rank == rank_ref[:, j : j + 1] + first_rank, 1.0, 0.0)
        slot_gate = jnp.dot(
            owner, weight, preferred_element_type=F32, precision=lax.Precision.HIGHEST
        )
        gslot[...] += jnp.broadcast_to(
            jnp.sum(chosen * slot_gate, axis=1, keepdims=True), (ROWS, TOK)
        )
        sel[:, j * TOK : (j + 1) * TOK] = chosen.astype(BF)
        selt[j * TOK : (j + 1) * TOK, :] = chosen.T.astype(BF)

    slots_of(0)
    slots_of(1)
    ag_next(0, 2)
    slots_of(7)
    slots_of(2)
    ag_next(0, 3)
    ag_next(1, 2)
    slots_of(6)
    slots_of(3)
    ag_first(2)
    ag_next(0, 4)
    ag_next(1, 3)
    slots_of(5)
    slots_of(4)

    def back(n):
        i, j = n // NY, n % NY
        return ((NX - i) % NX) * NY + (NY - j) % NY

    def disp_copy(u, n):
        m = back(n)
        return rc(sbuf.at[u, n], drecv.at[u, m], dss.at[u, n], dsr.at[u, m], at(n // NY, 0, n % NY))

    def ret_copy(u, n):
        m = back(n)
        return rc(sbuf.at[u, n], rrecv.at[u, m], rss.at[u, n], rsr.at[u, m], at(n // NY, 0, n % NY))

    def wide(lanes):
        return jnp.concatenate([lanes] * (FU // TOK), axis=1)

    def select(u):
        rows = nn(sel[...], ag[0, u].reshape(NZ * TOK, FU)).astype(BF)
        sbuf[u, :, :, 0:FU] = rows.reshape(PLANE, SEG, FU)
        cots = nn(sel[...], ag[1, u].reshape(NZ * TOK, FU))
        sgsel[u] = cots.astype(BF)
        scaled = (cots * wide(gslot[...])).astype(BF)
        sbuf[u, :, :, FU:] = scaled.reshape(PLANE, SEG, FU)
        drecv[u, 0] = sbuf[u, 0]

        for n in ORDER:
            disp_copy(u, n).start()

    def wait_weights():
        for copy in local_weights():
            copy.wait()
        for copy in sibling_weights():
            copy.wait_send()
        other = pl.ds(pl.multiple_of((1 - r) * HALF, 128), HALF)
        rc(wg_hbm, wg.at[:, other], wss.at[0], wrs.at[0], sib).wait_recv()
        rc(wu_hbm, wu.at[:, other], wss.at[1], wrs.at[1], sib).wait_recv()
        rc(wd_hbm, wd.at[other, :], wss.at[2], wrs.at[2], sib).wait_recv()

    def gather_rows(u):
        @pl.loop(1, PLANE)
        def _(n):
            disp_copy(u, n).wait_recv()

    def project(u, c, parts):
        size, count = ROWS // parts, PLANE // parts
        feats = pl.ds(pl.multiple_of(u * FU, FU), FU)
        part = pl.ds(pl.multiple_of(c * size, size), size)
        chips = pl.ds(c * count, count)
        rows = drecv[u, chips, :, 0:FU].reshape(size, FU)
        acc[0, part, :] += nn(rows, wg[feats, :])
        acc[1, part, :] += nn(rows, wu[feats, :])
        cots = drecv[u, chips, :, FU:].reshape(size, FU)
        acc[2, part, :] += nt(cots, wd[:, feats])

    def project_all(u):
        gather_rows(u)

        project(u, 0, 1)

    def activate(c):
        @pl.loop(0, PROWS // 80)
        def _(k):
            part = pl.ds(pl.multiple_of(c * PROWS + k * 80, 16), 80)
            gate_pre, up_pre, grad = acc[0, part, :], acc[1, part, :], acc[2, part, :]
            sig = jax.nn.sigmoid(gate_pre)
            swish = gate_pre * sig
            hid[part, :] = (swish * up_pre).astype(BF)
            ggr[part, :] = (grad * up_pre * sig * (1.0 + gate_pre * (1.0 - sig))).astype(BF)
            ugr[part, :] = (grad * swish).astype(BF)

    def answer(u, c, parts):
        size, count = ROWS // parts, PLANE // parts
        feats = pl.ds(pl.multiple_of(u * FU, FU), FU)
        part = pl.ds(pl.multiple_of(c * size, size), size)
        chips = pl.ds(c * count, count)
        outs = nn(hid[part, :], wd[:, feats]).astype(BF)
        sbuf[u, chips, :, 0:FU] = outs.reshape(count, SEG, FU)
        grads = (nt(ggr[part, :], wg[feats, :]) + nt(ugr[part, :], wu[feats, :])).astype(BF)
        sbuf[u, chips, :, FU:] = grads.reshape(count, SEG, FU)

        @pl.loop(0, count)
        def _(k):
            n = (c + 1) * count - 1 - k

            @pl.when(n > 0)
            def _():
                ret_copy(u, n).start()

    def answer_all(u):
        answer(u, 0, 1)

        rrecv[u, 0] = sbuf[u, 0]

    @pl.loop(0, UNITS)
    def _(u):
        @pl.when(u + 1 < UNITS)
        def _():
            ag_next(u + 1, 4)

        ag_copy(u, 0, 4).wait_recv()
        ag_copy(u, 1, 4).wait_recv()
        sib_copy(u, 4).start()

        @pl.when(u + 2 < UNITS)
        def _():
            ag_next(u + 2, 2)

        for j in range(1, NZ):
            sib_wait(u, j).wait_recv()
        select(u)

        @pl.when(u + 2 < UNITS)
        def _():
            ag_next(u + 2, 3)

        @pl.when(u + 3 < UNITS)
        def _():
            ag_first(u + 3)

        @pl.when(u == 0)
        def _():
            sibling_weights()[1].start()

        @pl.when(u == 1)
        def _():
            sibling_weights()[2].start()

        @pl.when(u == LAG)
        def _():
            wait_weights()

        @pl.when(u >= LAG)
        def _():
            project_all(u - LAG)

    @pl.loop(0, UNITS)
    def _(u):
        for step in range(1, 5):
            ag_copy(u, 0, step).wait_send()
            ag_copy(u, 1, step).wait_send()
        for j in range(1, NZ):
            sib_copy(u, j).wait_send()

    pl.semaphore_signal(free, inc=1, device_id=sib, device_id_type=MESH)

    @pl.loop(UNITS - LAG, UNITS - 1)
    def _(u):
        project_all(u)

    @pl.loop(0, UNITS)
    def _(u):
        @pl.loop(1, PLANE)
        def _(n):
            disp_copy(u, n).wait_send()

    gather_rows(UNITS - 1)

    @pl.loop(0, PARTS)
    def _(c):
        project(UNITS - 1, c, PARTS)
        activate(c)
        answer(0, c, PARTS)

    rrecv[0, 0] = sbuf[0, 0]

    @pl.loop(1, AHEAD)
    def _(u):
        answer_all(u)

    for k in range(FF // TOK):
        cols = slice(k * TOK, (k + 1) * TOK)
        hidt[cols, :] = hid[:, cols].astype(F32).T.astype(BF)

    def wd_copy(u):
        return rc(wsend.at[u], wrecv.at[u], wgs.at[u], wgr.at[u], sib)

    def wd_other(u):
        half = hidt[pl.ds(pl.multiple_of((1 - r) * HALF, HALF), HALF), :]
        wsend[u] = nn(half, drecv[u, :, :, FU:].reshape(ROWS, FU)).astype(BF)
        wd_copy(u).start()

    def wd_out(u):
        feats = pl.ds(pl.multiple_of(u * FU, FU), FU)
        return pltpu.make_async_copy(wsend.at[u], wdg_hbm.at[:, feats], wos.at[u])

    def wd_mine(u):
        half = hidt[pl.ds(pl.multiple_of(r * HALF, HALF), HALF), :]
        part = nn(half, drecv[u, :, :, FU:].reshape(ROWS, FU))
        wd_copy(u).wait_recv()
        wd_copy(u).wait_send()
        wsend[u] = (part + wrecv[u].astype(F32)).astype(BF)
        wd_out(u).start()

    def t_copy(u):
        return rc(ag.at[0, u], ag.at[1, u], ts.at[u], tr.at[u], sib)

    pl.semaphore_wait(free, 1)

    def combine_other(u):
        @pl.loop(1, PLANE)
        def _(n):
            ret_copy(u, n).wait_recv()

        outs = rrecv[u, :, :, 0:FU].astype(F32).reshape(ROWS, FU)
        terms = outs * sgsel[u].astype(F32)
        for k in range(FU // TOK):
            dots[...] += terms[:, k * TOK : (k + 1) * TOK]
        rrecv[u, :, :, 0:FU] = (outs * wide(gslot[...])).astype(BF).reshape(PLANE, SEG, FU)

        kept = rrecv[u, :, :, pl.ds(pl.multiple_of((1 - r) * FU, FU), FU)].reshape(ROWS, FU)

        ag[0, u] = nn(selt[...], kept).astype(BF).reshape(NZ, TOK, FU)
        t_copy(u).start()

    def combine_mine(u):
        t_copy(u).wait_recv()
        kept = rrecv[u, :, :, pl.ds(pl.multiple_of(r * FU, FU), FU)].reshape(ROWS, FU)

        total = nn(selt[...], kept).reshape(NZ, TOK, FU) + ag[1, u].astype(F32)
        ag[1, u] = total.astype(BF)

    def rs_copy(u, way, step):
        sign = 1 - 2 * way
        src = 5 - step if way == 0 else step + 3
        cols = slice(None)
        if step == 1:
            cols = slice(0, HU) if way == 0 else slice(HU, FU)
        return rc(
            ag.at[1, u, src, :, cols], rsrecv.at[u, way, step - 1, :, cols],
            qs.at[u, way, step - 1], qr.at[u, way, step - 1], at(0, sign, 0),
        )

    def rs_next(u, step):
        for way in range(2):
            rs_copy(u, way, step - 1).wait_recv()
            src = 5 - step if way == 0 else step + 3
            cols = slice(0, FU)
            if step == 2:
                cols = slice(0, HU) if way == 0 else slice(HU, FU)
            ag[1, u, src, :, cols] = (
                ag[1, u, src, :, cols].astype(F32)
                + rsrecv[u, way, step - 2, :, cols].astype(F32)
            ).astype(BF)
            rs_copy(u, way, step).start()

    def dots_copy(d):
        return rc(dbuf.at[d], drx.at[NZ - d], ds_.at[d], dr_.at[NZ - d], at(0, d, 0))

    def tot_part(u):
        return acc.at[u % 2, pl.ds(pl.multiple_of(u // 2 * TOK, TOK), TOK), 0:FU]

    def tot_copy(u):
        return pltpu.make_async_copy(tot_part(u), tot_hbm.at[r, u], tl.at[u])

    def tot_send(u):
        return rc(tot_part(u), tot_hbm.at[r, u], tss.at[u], trs.at[u], sib)

    def tot_wait(u):
        return rc(tot_part(u), tot_hbm.at[1 - r, u], tss.at[u], trs.at[u], sib)

    gg_copy = rc(ggx.at[0], ggx.at[1], es.at[0], er.at[0], sib)

    @pl.loop(0, UNITS + 5)
    def _(p):
        @pl.when(p >= 5)
        def _():
            u = p - 5
            rs_copy(u, 0, 4).wait_recv()
            rs_copy(u, 1, 4).wait_recv()
            acc[u % 2, pl.ds(pl.multiple_of(u // 2 * TOK, TOK), TOK), 0:FU] = (
                ag[1, u, 0].astype(F32)
                + rsrecv[u, 0, 3].astype(F32)
                + rsrecv[u, 1, 3].astype(F32)
            )
            tot_copy(u).start()
            tot_send(u).start()

        for step in (4, 3, 2):
            @pl.when((p >= step) & (p < UNITS + step))
            def _(step=step):
                rs_next(p - step, step)

        @pl.when((p >= 1) & (p < UNITS + 1))
        def _():
            u = p - 1
            combine_mine(u)
            rs_copy(u, 0, 1).start()
            rs_copy(u, 1, 1).start()

        @pl.when(p + AHEAD < UNITS)
        def _():
            answer_all(p + AHEAD)

        @pl.when(p < UNITS)
        def _():
            wd_other(p)

        @pl.when((p >= 1) & (p < UNITS + 1))
        def _():
            wd_mine(p - 1)

        @pl.when(p < UNITS)
        def _():
            combine_other(p)

        @pl.when(p == UNITS - 1)
        def _():
            by_owner = owner_ref[...] * jnp.sum(dots[...], axis=1, keepdims=True)
            for j in range(NZ):
                dbuf[j] = lax.dot_general(
                    by_owner, sel[:, j * TOK : (j + 1) * TOK].astype(F32),
                    (((0,), (0,)), ((), ())),
                    preferred_element_type=F32, precision=lax.Precision.HIGHEST,
                )

            @pl.loop(1, NZ)
            def _(d):
                dots_copy(d).start()

        @pl.when(p == UNITS + 2)
        def _():
            drx[0] = dbuf[0]

            @pl.loop(1, NZ)
            def _(d):
                dots_copy(d).wait_recv()

            ids_t = meta[0, 0:TOP]
            rows = []
            for k in range(TOP):
                got = jnp.zeros((PLANE, TOK), F32)
                for m in range(NZ):
                    plane = z + m
                    plane = jnp.where(plane >= NZ, plane - NZ, plane)
                    got = got + jnp.where(ids_t[k : k + 1, :] == experts_of(plane), drx[m], 0.0)
                rows.append(jnp.sum(got, axis=0, keepdims=True))
            ggx[0] = jnp.concatenate(rows, axis=0)
            gg_copy.start()

    @pl.loop(0, UNITS)
    def _(u):
        @pl.loop(1, PLANE)
        def _(n):
            ret_copy(u, n).wait_send()

        for step in range(1, 5):
            rs_copy(u, 0, step).wait_send()
            rs_copy(u, 1, step).wait_send()
        t_copy(u).wait_send()
        wd_out(u).wait()
        tot_copy(u).wait()
        tot_send(u).wait_send()
        tot_wait(u).wait_recv()

    @pl.loop(1, NZ)
    def _(d):
        dots_copy(d).wait_send()
        meta_copy(d).wait_send()

    gg_copy.wait()
    gg_ref[...] = ggx[0] + ggx[1]


def finish(
    tot, first_ref, second_ref, gain_ref, gates_in, wd_in,
    inv_ref, fg_ref, gg_ref, wd_ref,
):
    wd_ref[...] = wd_in[...]
    gg_ref[...] = gates_in[...]
    values = first_ref[...].astype(F32)
    inverse = lax.rsqrt(jnp.mean(values * values, axis=1, keepdims=True) + EPSILON)
    gain = gain_ref[...].astype(F32)
    along = jnp.zeros((TOK, 1), F32)
    for u in range(UNITS):
        cols = slice(u * FU, (u + 1) * FU)
        inv_ref[:, cols] = (second_ref[:, cols].astype(F32) - tot[0, u]).astype(BF)
        along = along + jnp.sum(tot[1, u] * gain[:, cols] * values[:, cols], axis=1, keepdims=True)
    shift = inverse * inverse * inverse * (along / WIDTH)
    for u in range(UNITS):
        cols = slice(u * FU, (u + 1) * FU)
        fg_ref[:, cols] = (
            inverse * (tot[1, u] * gain[:, cols]) - values[:, cols] * shift
        ).astype(BF)


def slot_tables():
    slot = np.arange(ROWS)
    owner = (slot[:, None] // SEG == np.arange(PLANE)[None, :]).astype(np.float32)
    block, order = slot % SEG // SHARE, slot % SHARE
    rank = np.where(block[:, None] == np.arange(NZ)[None, :], order[:, None], -100)
    return owner, rank.astype(np.float32)


def local(first, second, cot, gain, ids, gates, w_gate, w_up, w_down):
    owner, rank = slot_tables()
    vmem = pl.BlockSpec(memory_space=pltpu.VMEM)
    hbm = pl.BlockSpec(memory_space=pl.ANY)
    dma = pltpu.SemaphoreType.DMA
    gain = gain.reshape(1, WIDTH)
    tot, gg, wdg = pl.pallas_call(
        kernel,
        out_shape=(
            jax.ShapeDtypeStruct((2, UNITS, TOK, FU), F32),
            jax.ShapeDtypeStruct((TOP, TOK), F32),
            jax.ShapeDtypeStruct((HALF, WIDTH), BF),
        ),
        in_specs=[vmem] * 7 + [hbm] * 3,
        out_specs=(hbm, vmem, hbm),
        scratch_shapes=[
            pltpu.VMEM((WIDTH, FF), BF),
            pltpu.VMEM((WIDTH, FF), BF),
            pltpu.VMEM((FF, WIDTH), BF),
            pltpu.VMEM((2, UNITS, NZ, TOK, FU), BF),
            pltpu.VMEM((NZ, 2 * TOP, TOK), F32),
            pltpu.VMEM((ROWS, NZ * TOK), BF),
            pltpu.VMEM((NZ * TOK, ROWS), BF),
            pltpu.VMEM((ROWS, TOK), F32),
            pltpu.VMEM((UNITS, ROWS, FU), BF),
            pltpu.VMEM((UNITS, PLANE, SEG, 2 * FU), BF),
            pltpu.VMEM((UNITS, PLANE, SEG, 2 * FU), BF),
            pltpu.VMEM((UNITS, PLANE, SEG, 2 * FU), BF),
            pltpu.VMEM((3, ROWS, FF), F32),
            pltpu.VMEM((ROWS, FF), BF),
            pltpu.VMEM((FF, ROWS), BF),
            pltpu.VMEM((ROWS, FF), BF),
            pltpu.VMEM((ROWS, FF), BF),
            pltpu.VMEM((UNITS, 2, 4, TOK, FU), BF),
            pltpu.VMEM((UNITS, HALF, FU), BF),
            pltpu.VMEM((UNITS, HALF, FU), BF),
            pltpu.VMEM((ROWS, TOK), F32),
            pltpu.VMEM((NZ, PLANE, TOK), F32),
            pltpu.VMEM((NZ, PLANE, TOK), F32),
            pltpu.VMEM((2, TOP, TOK), F32),
            dma((3,)), dma((3,)), dma((3,)),
            dma((UNITS, 2, 4)), dma((UNITS, 2, 4)),
            dma((UNITS, NZ)), dma((UNITS, NZ)),
            dma((NZ,)), dma((NZ,)),
            dma((UNITS, PLANE)), dma((UNITS, PLANE)),
            dma((UNITS, PLANE)), dma((UNITS, PLANE)),
            dma((UNITS,)), dma((UNITS,)),
            dma((UNITS, 2, 4)), dma((UNITS, 2, 4)),
            dma((UNITS,)), dma((UNITS,)),
            dma((NZ,)), dma((NZ,)),
            dma((1,)), dma((1,)), dma((UNITS,)),
            dma((UNITS,)), dma((UNITS,)), dma((UNITS,)), pltpu.SemaphoreType.REGULAR,
        ],
        compiler_params=pltpu.CompilerParams(
            collective_id=1, has_side_effects=True, vmem_limit_bytes=63 << 20
        ),
        name="experts_backward",
    )(
        first, cot, gain, ids.T, gates.T,
        jnp.asarray(owner), jnp.asarray(rank), w_gate[0], w_up[0], w_down[0],
    )
    inv, fg, gg, wdg = pl.pallas_call(
        finish,
        out_shape=(
            jax.ShapeDtypeStruct((TOK, WIDTH), BF),
            jax.ShapeDtypeStruct((TOK, WIDTH), BF),
            jax.ShapeDtypeStruct((TOP, TOK), F32),
            jax.ShapeDtypeStruct((HALF, WIDTH), BF),
        ),
        in_specs=[vmem] * 6,
        out_specs=(vmem,) * 4,
        compiler_params=pltpu.CompilerParams(vmem_limit_bytes=62 << 20),
        name="streams",
    )(tot, first, second, gain, gg, wdg)
    return inv, fg, gg.T, wdg[None]


def solution(mesh):
    rows = P("ep", None)
    return jax.shard_map(
        local,
        mesh=mesh,
        in_specs=(
            rows, rows, rows, P(), rows, rows,
            P("ep", None, "rep"), P("ep", None, "rep"), P("ep", "rep", None),
        ),
        out_specs=(rows, rows, rows, P("ep", "rep", None)),
        check_vma=False,
    )
```

```python
import jax
import jax.numpy as jnp
import numpy as np
from jax import lax
from jax.experimental import pallas as pl
from jax.experimental.pallas import tpu as pltpu
from jax.sharding import PartitionSpec as P

EPSILON = 1e-06
MESH = pl.DeviceIdType.MESH
BF = jnp.bfloat16
F32 = jnp.float32

NX, NZ, NY = 4, 8, 4
PLANE = NX * NY
TOK = 128
WIDTH = 2048
FF = 768
HALF = FF // 2
TOP = 8
SHARE = 5
SEG = NZ * SHARE
ROWS = PLANE * SEG
UNITS = 8
FU = WIDTH // UNITS
HU = FU // 2
PARTS = 2
PROWS, PCHIPS = ROWS // PARTS, PLANE // PARTS
AHEAD = 3
ORDER = (10, 6, 14, 9, 11, 5, 7, 13, 15, 2, 8, 1, 4, 3, 12)
LAG = 3


def nt(left, right):
    return lax.dot_general(left, right, (((1,), (1,)), ((), ())), preferred_element_type=F32)


def nn(left, right):
    return jnp.dot(left, right, preferred_element_type=F32)


def kernel(
    first_ref, cot_ref, gain_ref, ids_ref, gates_ref, owner_ref, rank_ref,
    wg_hbm, wu_hbm, wd_hbm,
    tot_hbm, gg_ref, wdg_hbm,
    wg, wu, wd, ag, meta, sel, selt, gslot, sgsel, sbuf, drecv, rrecv, acc, hid, hidt, ggr, ugr,
    rsrecv, wsend, wrecv, dots, dbuf, drx, ggx,
    wl_sem, wss, wrs, ags, agr, sbs, sbr, ms, mr, dss, dsr, rss, rsr, ts, tr, qs, qr,
    wgs, wgr, ds_, dr_, es, er, wos, tl, tss, trs, free,
):
    r = lax.axis_index("rep")
    ep = lax.axis_index("ep")
    x, z, y = ep // (NZ * NY), (ep // NY) % NZ, ep % NY

    def at(dx, dz, dy):
        return {"ep": (((x + dx) % NX) * NZ + (z + dz) % NZ) * NY + (y + dy) % NY}

    sib = {"rep": 1 - r}

    def rc(src, dst, send, recv, dev):
        return pltpu.make_async_remote_copy(
            src_ref=src, dst_ref=dst, send_sem=send, recv_sem=recv,
            device_id=dev, device_id_type=MESH,
        )

    barrier = pltpu.get_barrier_semaphore()
    pl.semaphore_signal(barrier, inc=1, device_id=sib, device_id_type=MESH)

    @pl.loop(1, NZ)
    def _(d):
        pl.semaphore_signal(barrier, inc=1, device_id=at(0, d, 0), device_id_type=MESH)

    @pl.loop(1, PLANE)
    def _(n):
        pl.semaphore_signal(barrier, inc=1, device_id=at(n // NY, 0, n % NY), device_id_type=MESH)

    def local_weights():
        cols = pl.ds(pl.multiple_of(r * HALF, 128), HALF)
        return [
            pltpu.make_async_copy(wg_hbm, wg.at[:, cols], wl_sem.at[0]),
            pltpu.make_async_copy(wu_hbm, wu.at[:, cols], wl_sem.at[1]),
            pltpu.make_async_copy(wd_hbm, wd.at[cols, :], wl_sem.at[2]),
        ]

    def sibling_weights():
        cols = pl.ds(pl.multiple_of(r * HALF, 128), HALF)
        return [
            rc(wg_hbm, wg.at[:, cols], wss.at[0], wrs.at[0], sib),
            rc(wu_hbm, wu.at[:, cols], wss.at[1], wrs.at[1], sib),
            rc(wd_hbm, wd.at[cols, :], wss.at[2], wrs.at[2], sib),
        ]

    for copy in local_weights():
        copy.start()

    values = first_ref[...].astype(F32)
    inverse = lax.rsqrt(jnp.mean(values * values, axis=1, keepdims=True) + EPSILON)
    normed = (values * inverse * gain_ref[...].astype(F32)).astype(BF)
    for u in range(UNITS):
        ag[0, u, 0] = normed[:, u * FU : (u + 1) * FU]
        ag[1, u, 0] = cot_ref[:, u * FU : (u + 1) * FU]
    meta[0, 0:TOP] = ids_ref[...].astype(F32)
    meta[0, TOP : 2 * TOP] = gates_ref[...]

    pl.semaphore_wait(barrier, NZ + PLANE - 1)

    def ag_copy(u, way, step):
        sign = 1 - 2 * way
        src = (NZ - (step - 1)) % NZ if way == 0 else step - 1
        dst = NZ - step if way == 0 else step
        cols = slice(None)
        if step == 4:
            cols = slice(0, HU) if way == 0 else slice(HU, FU)
        return rc(
            ag.at[r, u, src, :, cols], ag.at[r, u, dst, :, cols],
            ags.at[u, way, step - 1], agr.at[u, way, step - 1], at(0, sign, 0),
        )

    def sib_copy(u, j):
        return rc(ag.at[r, u, j], ag.at[r, u, j], sbs.at[u, j], sbr.at[u, j], sib)

    def sib_wait(u, j):
        return rc(ag.at[1 - r, u, j], ag.at[1 - r, u, j], sbs.at[u, j], sbr.at[u, j], sib)

    def ag_first(u):
        ag_copy(u, 0, 1).start()
        ag_copy(u, 1, 1).start()

    def ag_next(u, step):
        for way in range(2):
            ag_copy(u, way, step - 1).wait_recv()
            ag_copy(u, way, step).start()
        for j in (NZ - (step - 1), step - 1):
            sib_copy(u, j).start()

    ag_first(0)


    def meta_copy(d):
        return rc(meta.at[0], meta.at[NZ - d], ms.at[d], mr.at[NZ - d], at(0, d, 0))

    @pl.loop(1, NZ)
    def _(d):
        meta_copy(d).start()

    ag_first(1)
    sibling_weights()[0].start()
    dots[...] = jnp.zeros_like(dots)

    d_index = lax.broadcasted_iota(jnp.int32, (PLANE, 1), 0)
    dx, dy = d_index >> 2, d_index & 3
    ex, ey = x + dx, y + dy
    ex = jnp.where(ex >= NX, ex - NX, ex)
    ey = jnp.where(ey >= NY, ey - NY, ey)

    def experts_of(plane):
        return ((ex * NZ + plane) * NY + ey).astype(F32)

    experts = experts_of(z)
    before = (
        lax.broadcasted_iota(jnp.int32, (TOK, TOK), 0)
        < lax.broadcasted_iota(jnp.int32, (TOK, TOK), 1)
    ).astype(BF)
    gslot[...] = jnp.zeros_like(gslot)
    owner = owner_ref[...]
    first_rank = (r * SHARE).astype(F32)

    def slots_of(j):
        if j:
            meta_copy(NZ - j).wait_recv()
        hits = jnp.zeros((PLANE, TOK), F32)
        weight = jnp.zeros((PLANE, TOK), F32)
        for k in range(TOP):
            match = meta[j, k : k + 1, :] == experts
            hits = hits + jnp.where(match, 1.0, 0.0)
            weight = weight + jnp.where(match, meta[j, TOP + k : TOP + k + 1, :], 0.0)
        rank = nn(hits.astype(BF), before)
        rank = jnp.where(hits > 0.0, rank, -1.0)
        slot_rank = nn(owner.astype(BF), rank.astype(BF))
        chosen = jnp.where(slot_rank == rank_ref[:, j : j + 1] + first_rank, 1.0, 0.0)
        slot_gate = jnp.dot(
            owner, weight, preferred_element_type=F32, precision=lax.Precision.HIGHEST
        )
        gslot[...] += jnp.broadcast_to(
            jnp.sum(chosen * slot_gate, axis=1, keepdims=True), (ROWS, TOK)
        )
        sel[:, j * TOK : (j + 1) * TOK] = chosen.astype(BF)
        selt[j * TOK : (j + 1) * TOK, :] = chosen.T.astype(BF)

    def ag_last(u):
        ag_copy(u, 0, 4).wait_recv()
        ag_copy(u, 1, 4).wait_recv()
        sib_copy(u, 4).start()

    slots_of(0)
    ag_next(0, 2)
    slots_of(1)
    slots_of(7)
    ag_next(0, 3)
    ag_next(1, 2)
    slots_of(2)
    slots_of(6)
    ag_first(2)
    ag_next(0, 4)
    ag_next(1, 3)
    slots_of(3)
    slots_of(5)
    slots_of(4)
    acc[...] = jnp.zeros_like(acc)
    ag_last(0)

    def back(n):
        i, j = n // NY, n % NY
        return ((NX - i) % NX) * NY + (NY - j) % NY

    def disp_copy(u, n):
        m = back(n)
        return rc(sbuf.at[u, n], drecv.at[u, m], dss.at[u, n], dsr.at[u, m], at(n // NY, 0, n % NY))

    def ret_copy(u, n):
        m = back(n)
        return rc(sbuf.at[u, n], rrecv.at[u, m], rss.at[u, n], rsr.at[u, m], at(n // NY, 0, n % NY))

    def wide(lanes):
        return jnp.concatenate([lanes] * (FU // TOK), axis=1)

    def select(u):
        rows = nn(sel[...], ag[0, u].reshape(NZ * TOK, FU)).astype(BF)
        sbuf[u, :, :, 0:FU] = rows.reshape(PLANE, SEG, FU)
        cots = nn(sel[...], ag[1, u].reshape(NZ * TOK, FU))
        sgsel[u] = cots.astype(BF)
        scaled = (cots * wide(gslot[...])).astype(BF)
        sbuf[u, :, :, FU:] = scaled.reshape(PLANE, SEG, FU)
        drecv[u, 0] = sbuf[u, 0]

        for n in ORDER:
            disp_copy(u, n).start()

    def wait_weights():
        for copy in local_weights():
            copy.wait()
        for copy in sibling_weights():
            copy.wait_send()
        other = pl.ds(pl.multiple_of((1 - r) * HALF, 128), HALF)
        rc(wg_hbm, wg.at[:, other], wss.at[0], wrs.at[0], sib).wait_recv()
        rc(wu_hbm, wu.at[:, other], wss.at[1], wrs.at[1], sib).wait_recv()
        rc(wd_hbm, wd.at[other, :], wss.at[2], wrs.at[2], sib).wait_recv()

    def gather_rows(u):
        @pl.loop(1, PLANE)
        def _(n):
            disp_copy(u, n).wait_recv()

    def project(u, c, parts):
        size, count = ROWS // parts, PLANE // parts
        feats = pl.ds(pl.multiple_of(u * FU, FU), FU)
        part = pl.ds(pl.multiple_of(c * size, size), size)
        chips = pl.ds(c * count, count)
        rows = drecv[u, chips, :, 0:FU].reshape(size, FU)
        acc[0, part, :] += nn(rows, wg[feats, :])
        acc[1, part, :] += nn(rows, wu[feats, :])
        cots = drecv[u, chips, :, FU:].reshape(size, FU)
        acc[2, part, :] += nt(cots, wd[:, feats])

    def project_all(u):
        gather_rows(u)

        project(u, 0, 1)

    def activate(c):
        @pl.loop(0, PROWS // 80)
        def _(k):
            part = pl.ds(pl.multiple_of(c * PROWS + k * 80, 16), 80)
            gate_pre, up_pre, grad = acc[0, part, :], acc[1, part, :], acc[2, part, :]
            sig = jax.nn.sigmoid(gate_pre)
            swish = gate_pre * sig
            hid[part, :] = (swish * up_pre).astype(BF)
            ggr[part, :] = (grad * up_pre * sig * (1.0 + gate_pre * (1.0 - sig))).astype(BF)
            ugr[part, :] = (grad * swish).astype(BF)

    def answer(u, c, parts):
        size, count = ROWS // parts, PLANE // parts
        feats = pl.ds(pl.multiple_of(u * FU, FU), FU)
        part = pl.ds(pl.multiple_of(c * size, size), size)
        chips = pl.ds(c * count, count)
        outs = nn(hid[part, :], wd[:, feats]).astype(BF)
        sbuf[u, chips, :, 0:FU] = outs.reshape(count, SEG, FU)
        grads = (nt(ggr[part, :], wg[feats, :]) + nt(ugr[part, :], wu[feats, :])).astype(BF)
        sbuf[u, chips, :, FU:] = grads.reshape(count, SEG, FU)

        @pl.loop(0, count)
        def _(k):
            n = (c + 1) * count - 1 - k

            @pl.when(n > 0)
            def _():
                ret_copy(u, n).start()

    def answer_all(u):
        answer(u, 0, 1)

        rrecv[u, 0] = sbuf[u, 0]

    @pl.loop(0, UNITS)
    def _(u):
        for j in range(1, NZ):
            sib_wait(u, j).wait_recv()
        select(u)

        @pl.when(u + 1 < UNITS)
        def _():
            ag_next(u + 1, 4)

        @pl.when(u + 2 < UNITS)
        def _():
            ag_next(u + 2, 2)

        @pl.when(u == 0)
        def _():
            sibling_weights()[1].start()

        @pl.when(u == 1)
        def _():
            sibling_weights()[2].start()

        @pl.when(u == LAG)
        def _():
            wait_weights()

        @pl.when(u >= LAG)
        def _():
            project_all(u - LAG)

        @pl.when(u + 1 < UNITS)
        def _():
            ag_last(u + 1)

        @pl.when(u + 2 < UNITS)
        def _():
            ag_next(u + 2, 3)

        @pl.when(u + 3 < UNITS)
        def _():
            ag_first(u + 3)

    @pl.loop(0, UNITS)
    def _(u):
        for step in range(1, 5):
            ag_copy(u, 0, step).wait_send()
            ag_copy(u, 1, step).wait_send()
        for j in range(1, NZ):
            sib_copy(u, j).wait_send()

    pl.semaphore_signal(free, inc=1, device_id=sib, device_id_type=MESH)

    @pl.loop(UNITS - LAG, UNITS - 1)
    def _(u):
        project_all(u)

    @pl.loop(0, UNITS)
    def _(u):
        @pl.loop(1, PLANE)
        def _(n):
            disp_copy(u, n).wait_send()

    gather_rows(UNITS - 1)

    @pl.loop(0, PARTS)
    def _(c):
        project(UNITS - 1, c, PARTS)
        activate(c)
        answer(0, c, PARTS)

    rrecv[0, 0] = sbuf[0, 0]

    @pl.loop(1, AHEAD)
    def _(u):
        answer_all(u)

    for k in range(FF // TOK):
        cols = slice(k * TOK, (k + 1) * TOK)
        hidt[cols, :] = hid[:, cols].astype(F32).T.astype(BF)

    def wd_copy(u):
        return rc(wsend.at[u], wrecv.at[u], wgs.at[u], wgr.at[u], sib)

    def wd_other(u):
        half = hidt[pl.ds(pl.multiple_of((1 - r) * HALF, HALF), HALF), :]
        wsend[u] = nn(half, drecv[u, :, :, FU:].reshape(ROWS, FU)).astype(BF)
        wd_copy(u).start()

    def wd_out(u):
        feats = pl.ds(pl.multiple_of(u * FU, FU), FU)
        return pltpu.make_async_copy(wsend.at[u], wdg_hbm.at[:, feats], wos.at[u])

    def wd_mine(u):
        half = hidt[pl.ds(pl.multiple_of(r * HALF, HALF), HALF), :]
        part = nn(half, drecv[u, :, :, FU:].reshape(ROWS, FU))
        wd_copy(u).wait_recv()
        wd_copy(u).wait_send()
        wsend[u] = (part + wrecv[u].astype(F32)).astype(BF)
        wd_out(u).start()

    def t_copy(u):
        return rc(ag.at[0, u], ag.at[1, u], ts.at[u], tr.at[u], sib)

    pl.semaphore_wait(free, 1)

    def combine_other(u):
        @pl.loop(1, PLANE)
        def _(n):
            ret_copy(u, n).wait_recv()

        outs = rrecv[u, :, :, 0:FU].astype(F32).reshape(ROWS, FU)
        terms = outs * sgsel[u].astype(F32)
        for k in range(FU // TOK):
            dots[...] += terms[:, k * TOK : (k + 1) * TOK]
        rrecv[u, :, :, 0:FU] = (outs * wide(gslot[...])).astype(BF).reshape(PLANE, SEG, FU)

        kept = rrecv[u, :, :, pl.ds(pl.multiple_of((1 - r) * FU, FU), FU)].reshape(ROWS, FU)

        ag[0, u] = nn(selt[...], kept).astype(BF).reshape(NZ, TOK, FU)
        t_copy(u).start()

    def combine_mine(u):
        t_copy(u).wait_recv()
        kept = rrecv[u, :, :, pl.ds(pl.multiple_of(r * FU, FU), FU)].reshape(ROWS, FU)

        total = nn(selt[...], kept).reshape(NZ, TOK, FU) + ag[1, u].astype(F32)
        ag[1, u] = total.astype(BF)

    def rs_copy(u, way, step):
        sign = 1 - 2 * way
        src = 5 - step if way == 0 else step + 3
        cols = slice(None)
        if step == 1:
            cols = slice(0, HU) if way == 0 else slice(HU, FU)
        return rc(
            ag.at[1, u, src, :, cols], rsrecv.at[u, way, step - 1, :, cols],
            qs.at[u, way, step - 1], qr.at[u, way, step - 1], at(0, sign, 0),
        )

    def rs_next(u, step):
        for way in range(2):
            rs_copy(u, way, step - 1).wait_recv()
            src = 5 - step if way == 0 else step + 3
            cols = slice(0, FU)
            if step == 2:
                cols = slice(0, HU) if way == 0 else slice(HU, FU)
            ag[1, u, src, :, cols] = (
                ag[1, u, src, :, cols].astype(F32)
                + rsrecv[u, way, step - 2, :, cols].astype(F32)
            ).astype(BF)
            rs_copy(u, way, step).start()

    def dots_copy(d):
        return rc(dbuf.at[d], drx.at[NZ - d], ds_.at[d], dr_.at[NZ - d], at(0, d, 0))

    def tot_part(u):
        return acc.at[u % 2, pl.ds(pl.multiple_of(u // 2 * TOK, TOK), TOK), 0:FU]

    def tot_copy(u):
        return pltpu.make_async_copy(tot_part(u), tot_hbm.at[r, u], tl.at[u])

    def tot_send(u):
        return rc(tot_part(u), tot_hbm.at[r, u], tss.at[u], trs.at[u], sib)

    def tot_wait(u):
        return rc(tot_part(u), tot_hbm.at[1 - r, u], tss.at[u], trs.at[u], sib)

    gg_copy = rc(ggx.at[0], ggx.at[1], es.at[0], er.at[0], sib)

    @pl.loop(0, UNITS + 5)
    def _(p):
        @pl.when(p >= 5)
        def _():
            u = p - 5
            rs_copy(u, 0, 4).wait_recv()
            rs_copy(u, 1, 4).wait_recv()
            acc[u % 2, pl.ds(pl.multiple_of(u // 2 * TOK, TOK), TOK), 0:FU] = (
                ag[1, u, 0].astype(F32)
                + rsrecv[u, 0, 3].astype(F32)
                + rsrecv[u, 1, 3].astype(F32)
            )
            tot_copy(u).start()
            tot_send(u).start()

        for step in (4, 3, 2):
            @pl.when((p >= step) & (p < UNITS + step))
            def _(step=step):
                rs_next(p - step, step)

        @pl.when((p >= 1) & (p < UNITS + 1))
        def _():
            u = p - 1
            combine_mine(u)
            rs_copy(u, 0, 1).start()
            rs_copy(u, 1, 1).start()

        @pl.when(p + AHEAD < UNITS)
        def _():
            answer_all(p + AHEAD)

        @pl.when(p < UNITS)
        def _():
            wd_other(p)

        @pl.when((p >= 1) & (p < UNITS + 1))
        def _():
            wd_mine(p - 1)

        @pl.when(p < UNITS)
        def _():
            combine_other(p)

        @pl.when(p == UNITS)
        def _():
            by_owner = owner_ref[...] * jnp.sum(dots[...], axis=1, keepdims=True)
            for j in range(NZ):
                dbuf[j] = lax.dot_general(
                    by_owner, sel[:, j * TOK : (j + 1) * TOK].astype(F32),
                    (((0,), (0,)), ((), ())),
                    preferred_element_type=F32, precision=lax.Precision.HIGHEST,
                )

            @pl.loop(1, NZ)
            def _(d):
                dots_copy(d).start()

        @pl.when(p == UNITS + 3)
        def _():
            drx[0] = dbuf[0]

            @pl.loop(1, NZ)
            def _(d):
                dots_copy(d).wait_recv()

            ids_t = meta[0, 0:TOP]
            rows = []
            for k in range(TOP):
                got = jnp.zeros((PLANE, TOK), F32)
                for m in range(NZ):
                    plane = z + m
                    plane = jnp.where(plane >= NZ, plane - NZ, plane)
                    got = got + jnp.where(ids_t[k : k + 1, :] == experts_of(plane), drx[m], 0.0)
                rows.append(jnp.sum(got, axis=0, keepdims=True))
            ggx[0] = jnp.concatenate(rows, axis=0)
            gg_copy.start()

    @pl.loop(0, UNITS)
    def _(u):
        @pl.loop(1, PLANE)
        def _(n):
            ret_copy(u, n).wait_send()

        for step in range(1, 5):
            rs_copy(u, 0, step).wait_send()
            rs_copy(u, 1, step).wait_send()
        t_copy(u).wait_send()
        wd_out(u).wait()
        tot_copy(u).wait()
        tot_send(u).wait_send()
        tot_wait(u).wait_recv()

    @pl.loop(1, NZ)
    def _(d):
        dots_copy(d).wait_send()
        meta_copy(d).wait_send()

    gg_copy.wait()
    gg_ref[...] = ggx[0] + ggx[1]


def finish(
    tot, first_ref, second_ref, gain_ref, gates_in, wd_in,
    inv_ref, fg_ref, gg_ref, wd_ref,
):
    wd_ref[...] = wd_in[...]
    gg_ref[...] = gates_in[...]
    values = first_ref[...].astype(F32)
    inverse = lax.rsqrt(jnp.mean(values * values, axis=1, keepdims=True) + EPSILON)
    gain = gain_ref[...].astype(F32)
    along = jnp.zeros((TOK, 1), F32)
    for u in range(UNITS):
        cols = slice(u * FU, (u + 1) * FU)
        inv_ref[:, cols] = (second_ref[:, cols].astype(F32) - tot[0, u]).astype(BF)
        along = along + jnp.sum(tot[1, u] * gain[:, cols] * values[:, cols], axis=1, keepdims=True)
    shift = inverse * inverse * inverse * (along / WIDTH)
    for u in range(UNITS):
        cols = slice(u * FU, (u + 1) * FU)
        fg_ref[:, cols] = (
            inverse * (tot[1, u] * gain[:, cols]) - values[:, cols] * shift
        ).astype(BF)


def slot_tables():
    slot = np.arange(ROWS)
    owner = (slot[:, None] // SEG == np.arange(PLANE)[None, :]).astype(np.float32)
    block, order = slot % SEG // SHARE, slot % SHARE
    rank = np.where(block[:, None] == np.arange(NZ)[None, :], order[:, None], -100)
    return owner, rank.astype(np.float32)


def local(first, second, cot, gain, ids, gates, w_gate, w_up, w_down):
    owner, rank = slot_tables()
    vmem = pl.BlockSpec(memory_space=pltpu.VMEM)
    hbm = pl.BlockSpec(memory_space=pl.ANY)
    dma = pltpu.SemaphoreType.DMA
    gain = gain.reshape(1, WIDTH)
    tot, gg, wdg = pl.pallas_call(
        kernel,
        out_shape=(
            jax.ShapeDtypeStruct((2, UNITS, TOK, FU), F32),
            jax.ShapeDtypeStruct((TOP, TOK), F32),
            jax.ShapeDtypeStruct((HALF, WIDTH), BF),
        ),
        in_specs=[vmem] * 7 + [hbm] * 3,
        out_specs=(hbm, vmem, hbm),
        scratch_shapes=[
            pltpu.VMEM((WIDTH, FF), BF),
            pltpu.VMEM((WIDTH, FF), BF),
            pltpu.VMEM((FF, WIDTH), BF),
            pltpu.VMEM((2, UNITS, NZ, TOK, FU), BF),
            pltpu.VMEM((NZ, 2 * TOP, TOK), F32),
            pltpu.VMEM((ROWS, NZ * TOK), BF),
            pltpu.VMEM((NZ * TOK, ROWS), BF),
            pltpu.VMEM((ROWS, TOK), F32),
            pltpu.VMEM((UNITS, ROWS, FU), BF),
            pltpu.VMEM((UNITS, PLANE, SEG, 2 * FU), BF),
            pltpu.VMEM((UNITS, PLANE, SEG, 2 * FU), BF),
            pltpu.VMEM((UNITS, PLANE, SEG, 2 * FU), BF),
            pltpu.VMEM((3, ROWS, FF), F32),
            pltpu.VMEM((ROWS, FF), BF),
            pltpu.VMEM((FF, ROWS), BF),
            pltpu.VMEM((ROWS, FF), BF),
            pltpu.VMEM((ROWS, FF), BF),
            pltpu.VMEM((UNITS, 2, 4, TOK, FU), BF),
            pltpu.VMEM((UNITS, HALF, FU), BF),
            pltpu.VMEM((UNITS, HALF, FU), BF),
            pltpu.VMEM((ROWS, TOK), F32),
            pltpu.VMEM((NZ, PLANE, TOK), F32),
            pltpu.VMEM((NZ, PLANE, TOK), F32),
            pltpu.VMEM((2, TOP, TOK), F32),
            dma((3,)), dma((3,)), dma((3,)),
            dma((UNITS, 2, 4)), dma((UNITS, 2, 4)),
            dma((UNITS, NZ)), dma((UNITS, NZ)),
            dma((NZ,)), dma((NZ,)),
            dma((UNITS, PLANE)), dma((UNITS, PLANE)),
            dma((UNITS, PLANE)), dma((UNITS, PLANE)),
            dma((UNITS,)), dma((UNITS,)),
            dma((UNITS, 2, 4)), dma((UNITS, 2, 4)),
            dma((UNITS,)), dma((UNITS,)),
            dma((NZ,)), dma((NZ,)),
            dma((1,)), dma((1,)), dma((UNITS,)),
            dma((UNITS,)), dma((UNITS,)), dma((UNITS,)), pltpu.SemaphoreType.REGULAR,
        ],
        compiler_params=pltpu.CompilerParams(
            collective_id=1, has_side_effects=True, vmem_limit_bytes=63 << 20
        ),
        name="experts_backward",
    )(
        first, cot, gain, ids.T, gates.T,
        jnp.asarray(owner), jnp.asarray(rank), w_gate[0], w_up[0], w_down[0],
    )
    inv, fg, gg, wdg = pl.pallas_call(
        finish,
        out_shape=(
            jax.ShapeDtypeStruct((TOK, WIDTH), BF),
            jax.ShapeDtypeStruct((TOK, WIDTH), BF),
            jax.ShapeDtypeStruct((TOP, TOK), F32),
            jax.ShapeDtypeStruct((HALF, WIDTH), BF),
        ),
        in_specs=[vmem] * 6,
        out_specs=(vmem,) * 4,
        compiler_params=pltpu.CompilerParams(vmem_limit_bytes=62 << 20),
        name="streams",
    )(tot, first, second, gain, gg, wdg)
    return inv, fg, gg.T, wdg[None]


def solution(mesh):
    rows = P("ep", None)
    return jax.shard_map(
        local,
        mesh=mesh,
        in_specs=(
            rows, rows, rows, P(), rows, rows,
            P("ep", None, "rep"), P("ep", None, "rep"), P("ep", "rep", None),
        ),
        out_specs=(rows, rows, rows, P("ep", "rep", None)),
        check_vma=False,
    )
```

```python
import jax
import jax.numpy as jnp
import numpy as np
from jax import lax
from jax.experimental import pallas as pl
from jax.experimental.pallas import tpu as pltpu
from jax.sharding import PartitionSpec as P

EPSILON = 1e-06
MESH = pl.DeviceIdType.MESH
BF = jnp.bfloat16
F32 = jnp.float32

NX, NZ, NY = 4, 8, 4
PLANE = NX * NY
TOK = 128
WIDTH = 2048
FF = 768
HALF = FF // 2
TOP = 8
SHARE = 5
SEG = NZ * SHARE
ROWS = PLANE * SEG
UNITS = 8
FU = WIDTH // UNITS
HU = FU // 2
PARTS = 2
PROWS, PCHIPS = ROWS // PARTS, PLANE // PARTS
AHEAD = 3
ORDER = (10, 6, 14, 9, 11, 5, 7, 13, 15, 2, 8, 1, 4, 3, 12)
LAG = 3


def nt(left, right):
    return lax.dot_general(left, right, (((1,), (1,)), ((), ())), preferred_element_type=F32)


def nn(left, right):
    return jnp.dot(left, right, preferred_element_type=F32)


def kernel(
    first_ref, cot_ref, gain_ref, ids_ref, gates_ref, owner_ref, rank_ref,
    wg_hbm, wu_hbm, wd_hbm,
    tot_hbm, gg_ref, wdg_hbm,
    wg, wu, wd, ag, meta, sel, selt, gslot, sgsel, sbuf, drecv, rrecv, acc, hid, hidt, ggr, ugr,
    rsrecv, wsend, wrecv, dots, dbuf, drx, ggx,
    wl_sem, wss, wrs, ags, agr, sbs, sbr, ms, mr, dss, dsr, rss, rsr, ts, tr, qs, qr,
    wgs, wgr, ds_, dr_, es, er, wos, tl, tss, trs, free,
):
    r = lax.axis_index("rep")
    ep = lax.axis_index("ep")
    x, z, y = ep // (NZ * NY), (ep // NY) % NZ, ep % NY

    def at(dx, dz, dy):
        return {"ep": (((x + dx) % NX) * NZ + (z + dz) % NZ) * NY + (y + dy) % NY}

    sib = {"rep": 1 - r}

    def rc(src, dst, send, recv, dev):
        return pltpu.make_async_remote_copy(
            src_ref=src, dst_ref=dst, send_sem=send, recv_sem=recv,
            device_id=dev, device_id_type=MESH,
        )

    barrier = pltpu.get_barrier_semaphore()
    pl.semaphore_signal(barrier, inc=1, device_id=sib, device_id_type=MESH)

    @pl.loop(1, NZ)
    def _(d):
        pl.semaphore_signal(barrier, inc=1, device_id=at(0, d, 0), device_id_type=MESH)

    @pl.loop(1, PLANE)
    def _(n):
        pl.semaphore_signal(barrier, inc=1, device_id=at(n // NY, 0, n % NY), device_id_type=MESH)

    def local_weights():
        cols = pl.ds(pl.multiple_of(r * HALF, 128), HALF)
        return [
            pltpu.make_async_copy(wg_hbm, wg.at[:, cols], wl_sem.at[0]),
            pltpu.make_async_copy(wu_hbm, wu.at[:, cols], wl_sem.at[1]),
            pltpu.make_async_copy(wd_hbm, wd.at[cols, :], wl_sem.at[2]),
        ]

    def sibling_weights():
        cols = pl.ds(pl.multiple_of(r * HALF, 128), HALF)
        return [
            rc(wg_hbm, wg.at[:, cols], wss.at[0], wrs.at[0], sib),
            rc(wu_hbm, wu.at[:, cols], wss.at[1], wrs.at[1], sib),
            rc(wd_hbm, wd.at[cols, :], wss.at[2], wrs.at[2], sib),
        ]

    for copy in local_weights():
        copy.start()

    values = first_ref[...].astype(F32)
    inverse = lax.rsqrt(jnp.mean(values * values, axis=1, keepdims=True) + EPSILON)
    normed = (values * inverse * gain_ref[...].astype(F32).reshape(1, WIDTH)).astype(BF)
    for u in range(UNITS):
        ag[0, u, 0] = normed[:, u * FU : (u + 1) * FU]
        ag[1, u, 0] = cot_ref[:, u * FU : (u + 1) * FU]
    meta[0, 0:TOP] = ids_ref[...].astype(F32)
    meta[0, TOP : 2 * TOP] = gates_ref[...]

    pl.semaphore_wait(barrier, NZ + PLANE - 1)

    def ag_copy(u, way, step):
        sign = 1 - 2 * way
        src = (NZ - (step - 1)) % NZ if way == 0 else step - 1
        dst = NZ - step if way == 0 else step
        cols = slice(None)
        if step == 4:
            cols = slice(0, HU) if way == 0 else slice(HU, FU)
        return rc(
            ag.at[r, u, src, :, cols], ag.at[r, u, dst, :, cols],
            ags.at[u, way, step - 1], agr.at[u, way, step - 1], at(0, sign, 0),
        )

    runs = (pl.ds(1, 3), pl.ds(5, 3), pl.ds(4, 1))

    def sib_copy(u, k):
        part = ag.at[r, u, runs[k]]
        return rc(part, part, sbs.at[u, k], sbr.at[u, k], sib)

    def sib_wait(u, k):
        part = ag.at[1 - r, u, runs[k]]
        return rc(part, part, sbs.at[u, k], sbr.at[u, k], sib)

    def ag_first(u):
        ag_copy(u, 0, 1).start()
        ag_copy(u, 1, 1).start()

    def ag_next(u, step):
        for way in range(2):
            ag_copy(u, way, step - 1).wait_recv()
            ag_copy(u, way, step).start()
        if step == 4:
            sib_copy(u, 0).start()
            sib_copy(u, 1).start()

    ag_first(0)


    def meta_copy(d):
        return rc(meta.at[0], meta.at[NZ - d], ms.at[d], mr.at[NZ - d], at(0, d, 0))

    @pl.loop(1, NZ)
    def _(d):
        meta_copy(d).start()

    ag_first(1)
    sibling_weights()[0].start()
    dots[...] = jnp.zeros_like(dots)

    d_index = lax.broadcasted_iota(jnp.int32, (PLANE, 1), 0)
    dx, dy = d_index >> 2, d_index & 3
    ex, ey = x + dx, y + dy
    ex = jnp.where(ex >= NX, ex - NX, ex)
    ey = jnp.where(ey >= NY, ey - NY, ey)

    def experts_of(plane):
        return ((ex * NZ + plane) * NY + ey).astype(F32)

    experts = experts_of(z)
    before = (
        lax.broadcasted_iota(jnp.int32, (TOK, TOK), 0)
        < lax.broadcasted_iota(jnp.int32, (TOK, TOK), 1)
    ).astype(BF)
    gslot[...] = jnp.zeros_like(gslot)
    owner = owner_ref[...]
    first_rank = (r * SHARE).astype(F32)

    def slots_of(j):
        if j:
            meta_copy(NZ - j).wait_recv()
        hits = jnp.zeros((PLANE, TOK), F32)
        weight = jnp.zeros((PLANE, TOK), F32)
        for k in range(TOP):
            match = meta[j, k : k + 1, :] == experts
            hits = hits + jnp.where(match, 1.0, 0.0)
            weight = weight + jnp.where(match, meta[j, TOP + k : TOP + k + 1, :], 0.0)
        rank = nn(hits.astype(BF), before)
        rank = jnp.where(hits > 0.0, rank, -1.0)
        slot_rank = nn(owner.astype(BF), rank.astype(BF))
        chosen = jnp.where(slot_rank == rank_ref[:, j : j + 1] + first_rank, 1.0, 0.0)
        slot_gate = jnp.dot(
            owner, weight, preferred_element_type=F32, precision=lax.Precision.HIGHEST
        )
        gslot[...] += jnp.broadcast_to(
            jnp.sum(chosen * slot_gate, axis=1, keepdims=True), (ROWS, TOK)
        )
        sel[:, j * TOK : (j + 1) * TOK] = chosen.astype(BF)
        selt[j * TOK : (j + 1) * TOK, :] = chosen.T.astype(BF)

    def ag_last(u):
        ag_copy(u, 0, 4).wait_recv()
        ag_copy(u, 1, 4).wait_recv()
        sib_copy(u, 2).start()

    slots_of(0)
    ag_next(0, 2)
    slots_of(1)
    slots_of(7)
    ag_next(0, 3)
    ag_next(1, 2)
    slots_of(2)
    slots_of(6)
    ag_first(2)
    ag_next(0, 4)
    ag_next(1, 3)
    slots_of(3)
    slots_of(5)
    slots_of(4)
    acc[...] = jnp.zeros_like(acc)
    ag_last(0)

    def back(n):
        i, j = n // NY, n % NY
        return ((NX - i) % NX) * NY + (NY - j) % NY

    def disp_copy(u, n):
        m = back(n)
        return rc(sbuf.at[u, n], drecv.at[u, m], dss.at[u, n], dsr.at[u, m], at(n // NY, 0, n % NY))

    def ret_copy(u, n):
        m = back(n)
        return rc(sbuf.at[u, n], rrecv.at[u, m], rss.at[u, n], rsr.at[u, m], at(n // NY, 0, n % NY))

    def wide(lanes):
        return jnp.concatenate([lanes] * (FU // TOK), axis=1)

    def select(u):
        rows = nn(sel[...], ag[0, u].reshape(NZ * TOK, FU)).astype(BF)
        sbuf[u, :, :, 0:FU] = rows.reshape(PLANE, SEG, FU)
        cots = nn(sel[...], ag[1, u].reshape(NZ * TOK, FU))
        sgsel[u] = cots.astype(BF)
        scaled = (cots * wide(gslot[...])).astype(BF)
        sbuf[u, :, :, FU:] = scaled.reshape(PLANE, SEG, FU)
        drecv[u, 0] = sbuf[u, 0]

        for n in ORDER:
            disp_copy(u, n).start()

    def wait_weights():
        for copy in local_weights():
            copy.wait()
        for copy in sibling_weights():
            copy.wait_send()
        other = pl.ds(pl.multiple_of((1 - r) * HALF, 128), HALF)
        rc(wg_hbm, wg.at[:, other], wss.at[0], wrs.at[0], sib).wait_recv()
        rc(wu_hbm, wu.at[:, other], wss.at[1], wrs.at[1], sib).wait_recv()
        rc(wd_hbm, wd.at[other, :], wss.at[2], wrs.at[2], sib).wait_recv()

    def gather_rows(u):
        @pl.loop(1, PLANE)
        def _(n):
            disp_copy(u, n).wait_recv()

    def project(u, c, parts):
        size, count = ROWS // parts, PLANE // parts
        feats = pl.ds(pl.multiple_of(u * FU, FU), FU)
        part = pl.ds(pl.multiple_of(c * size, size), size)
        chips = pl.ds(c * count, count)
        rows = drecv[u, chips, :, 0:FU].reshape(size, FU)
        acc[0, part, :] += nn(rows, wg[feats, :])
        acc[1, part, :] += nn(rows, wu[feats, :])
        cots = drecv[u, chips, :, FU:].reshape(size, FU)
        acc[2, part, :] += nt(cots, wd[:, feats])

    def project_all(u):
        gather_rows(u)

        project(u, 0, 1)

    def activate(c):
        @pl.loop(0, PROWS // 80)
        def _(k):
            part = pl.ds(pl.multiple_of(c * PROWS + k * 80, 16), 80)
            gate_pre, up_pre, grad = acc[0, part, :], acc[1, part, :], acc[2, part, :]
            sig = jax.nn.sigmoid(gate_pre)
            swish = gate_pre * sig
            hid[part, :] = (swish * up_pre).astype(BF)
            ggr[part, :] = (grad * up_pre * sig * (1.0 + gate_pre * (1.0 - sig))).astype(BF)
            ugr[part, :] = (grad * swish).astype(BF)

    def answer(u, c, parts):
        size, count = ROWS // parts, PLANE // parts
        feats = pl.ds(pl.multiple_of(u * FU, FU), FU)
        part = pl.ds(pl.multiple_of(c * size, size), size)
        chips = pl.ds(c * count, count)
        outs = nn(hid[part, :], wd[:, feats]).astype(BF)
        sbuf[u, chips, :, 0:FU] = outs.reshape(count, SEG, FU)
        grads = (nt(ggr[part, :], wg[feats, :]) + nt(ugr[part, :], wu[feats, :])).astype(BF)
        sbuf[u, chips, :, FU:] = grads.reshape(count, SEG, FU)

        @pl.loop(0, count)
        def _(k):
            n = (c + 1) * count - 1 - k

            @pl.when(n > 0)
            def _():
                ret_copy(u, n).start()

    def answer_all(u):
        answer(u, 0, 1)

        rrecv[u, 0] = sbuf[u, 0]

    @pl.loop(0, UNITS)
    def _(u):
        for k in range(3):
            sib_wait(u, k).wait_recv()
        select(u)

        @pl.when(u + 1 < UNITS)
        def _():
            ag_next(u + 1, 4)

        @pl.when(u + 2 < UNITS)
        def _():
            ag_next(u + 2, 2)

        @pl.when(u == 0)
        def _():
            sibling_weights()[1].start()

        @pl.when(u == 1)
        def _():
            sibling_weights()[2].start()

        @pl.when(u == LAG)
        def _():
            wait_weights()

        @pl.when(u >= LAG)
        def _():
            project_all(u - LAG)

        @pl.when(u + 1 < UNITS)
        def _():
            ag_last(u + 1)

        @pl.when(u + 2 < UNITS)
        def _():
            ag_next(u + 2, 3)

        @pl.when(u + 3 < UNITS)
        def _():
            ag_first(u + 3)

    @pl.loop(0, UNITS)
    def _(u):
        for step in range(1, 5):
            ag_copy(u, 0, step).wait_send()
            ag_copy(u, 1, step).wait_send()
        for k in range(3):
            sib_copy(u, k).wait_send()

    pl.semaphore_signal(free, inc=1, device_id=sib, device_id_type=MESH)

    @pl.loop(UNITS - LAG, UNITS - 1)
    def _(u):
        project_all(u)

    @pl.loop(0, UNITS)
    def _(u):
        @pl.loop(1, PLANE)
        def _(n):
            disp_copy(u, n).wait_send()

    gather_rows(UNITS - 1)

    @pl.loop(0, PARTS)
    def _(c):
        project(UNITS - 1, c, PARTS)
        activate(c)
        answer(0, c, PARTS)

    rrecv[0, 0] = sbuf[0, 0]

    @pl.loop(1, AHEAD)
    def _(u):
        answer_all(u)

    for k in range(FF // TOK):
        cols = slice(k * TOK, (k + 1) * TOK)
        hidt[cols, :] = hid[:, cols].astype(F32).T.astype(BF)

    def wd_copy(u):
        return rc(wsend.at[u], wrecv.at[u], wgs.at[u], wgr.at[u], sib)

    def wd_other(u):
        half = hidt[pl.ds(pl.multiple_of((1 - r) * HALF, HALF), HALF), :]
        wsend[u] = nn(half, drecv[u, :, :, FU:].reshape(ROWS, FU)).astype(BF)
        wd_copy(u).start()

    def wd_out(u):
        feats = pl.ds(pl.multiple_of(u * FU, FU), FU)
        return pltpu.make_async_copy(wsend.at[u], wdg_hbm.at[:, feats], wos.at[u])

    def wd_mine(u):
        half = hidt[pl.ds(pl.multiple_of(r * HALF, HALF), HALF), :]
        part = nn(half, drecv[u, :, :, FU:].reshape(ROWS, FU))
        wd_copy(u).wait_recv()
        wd_copy(u).wait_send()
        wsend[u] = (part + wrecv[u].astype(F32)).astype(BF)
        wd_out(u).start()

    def t_copy(u):
        return rc(ag.at[0, u], ag.at[1, u], ts.at[u], tr.at[u], sib)

    pl.semaphore_wait(free, 1)

    def combine_other(u):
        @pl.loop(1, PLANE)
        def _(n):
            ret_copy(u, n).wait_recv()

        outs = rrecv[u, :, :, 0:FU].astype(F32).reshape(ROWS, FU)
        terms = outs * sgsel[u].astype(F32)
        for k in range(FU // TOK):
            dots[...] += terms[:, k * TOK : (k + 1) * TOK]
        rrecv[u, :, :, 0:FU] = (outs * wide(gslot[...])).astype(BF).reshape(PLANE, SEG, FU)

        kept = rrecv[u, :, :, pl.ds(pl.multiple_of((1 - r) * FU, FU), FU)].reshape(ROWS, FU)

        ag[0, u] = nn(selt[...], kept).astype(BF).reshape(NZ, TOK, FU)
        t_copy(u).start()

    def combine_mine(u):
        t_copy(u).wait_recv()
        kept = rrecv[u, :, :, pl.ds(pl.multiple_of(r * FU, FU), FU)].reshape(ROWS, FU)

        total = nn(selt[...], kept).reshape(NZ, TOK, FU) + ag[1, u].astype(F32)
        ag[1, u] = total.astype(BF)

    def rs_copy(u, way, step):
        sign = 1 - 2 * way
        src = 5 - step if way == 0 else step + 3
        cols = slice(None)
        if step == 1:
            cols = slice(0, HU) if way == 0 else slice(HU, FU)
        return rc(
            ag.at[1, u, src, :, cols], rsrecv.at[u, way, step - 1, :, cols],
            qs.at[u, way, step - 1], qr.at[u, way, step - 1], at(0, sign, 0),
        )

    def rs_next(u, step):
        for way in range(2):
            rs_copy(u, way, step - 1).wait_recv()
            src = 5 - step if way == 0 else step + 3
            cols = slice(0, FU)
            if step == 2:
                cols = slice(0, HU) if way == 0 else slice(HU, FU)
            ag[1, u, src, :, cols] = (
                ag[1, u, src, :, cols].astype(F32)
                + rsrecv[u, way, step - 2, :, cols].astype(F32)
            ).astype(BF)
            rs_copy(u, way, step).start()

    def dots_copy(d):
        return rc(dbuf.at[d], drx.at[NZ - d], ds_.at[d], dr_.at[NZ - d], at(0, d, 0))

    def tot_part(u):
        return acc.at[u % 2, pl.ds(pl.multiple_of(u // 2 * TOK, TOK), TOK), 0:FU]

    def tot_copy(u):
        return pltpu.make_async_copy(tot_part(u), tot_hbm.at[r, u], tl.at[u])

    def tot_send(u):
        return rc(tot_part(u), tot_hbm.at[r, u], tss.at[u], trs.at[u], sib)

    def tot_wait(u):
        return rc(tot_part(u), tot_hbm.at[1 - r, u], tss.at[u], trs.at[u], sib)

    gg_copy = rc(ggx.at[0], ggx.at[1], es.at[0], er.at[0], sib)

    @pl.loop(0, UNITS + 5)
    def _(p):
        @pl.when(p >= 5)
        def _():
            u = p - 5
            rs_copy(u, 0, 4).wait_recv()
            rs_copy(u, 1, 4).wait_recv()
            acc[u % 2, pl.ds(pl.multiple_of(u // 2 * TOK, TOK), TOK), 0:FU] = (
                ag[1, u, 0].astype(F32)
                + rsrecv[u, 0, 3].astype(F32)
                + rsrecv[u, 1, 3].astype(F32)
            )
            tot_copy(u).start()
            tot_send(u).start()

        for step in (4, 3, 2):
            @pl.when((p >= step) & (p < UNITS + step))
            def _(step=step):
                rs_next(p - step, step)

        @pl.when((p >= 1) & (p < UNITS + 1))
        def _():
            u = p - 1
            combine_mine(u)
            rs_copy(u, 0, 1).start()
            rs_copy(u, 1, 1).start()

        @pl.when(p + AHEAD < UNITS)
        def _():
            answer_all(p + AHEAD)

        @pl.when(p < UNITS)
        def _():
            wd_other(p)

        @pl.when((p >= 1) & (p < UNITS + 1))
        def _():
            wd_mine(p - 1)

        @pl.when(p < UNITS)
        def _():
            combine_other(p)

        @pl.when(p == UNITS)
        def _():
            by_owner = owner_ref[...] * jnp.sum(dots[...], axis=1, keepdims=True)
            for j in range(NZ):
                dbuf[j] = lax.dot_general(
                    by_owner, sel[:, j * TOK : (j + 1) * TOK].astype(F32),
                    (((0,), (0,)), ((), ())),
                    preferred_element_type=F32, precision=lax.Precision.HIGHEST,
                )

            @pl.loop(1, NZ)
            def _(d):
                dots_copy(d).start()

        @pl.when(p == UNITS + 3)
        def _():
            drx[0] = dbuf[0]

            @pl.loop(1, NZ)
            def _(d):
                dots_copy(d).wait_recv()

            ids_t = meta[0, 0:TOP]
            rows = []
            for k in range(TOP):
                got = jnp.zeros((PLANE, TOK), F32)
                for m in range(NZ):
                    plane = z + m
                    plane = jnp.where(plane >= NZ, plane - NZ, plane)
                    got = got + jnp.where(ids_t[k : k + 1, :] == experts_of(plane), drx[m], 0.0)
                rows.append(jnp.sum(got, axis=0, keepdims=True))
            ggx[0] = jnp.concatenate(rows, axis=0)
            gg_copy.start()

    @pl.loop(0, UNITS)
    def _(u):
        @pl.loop(1, PLANE)
        def _(n):
            ret_copy(u, n).wait_send()

        for step in range(1, 5):
            rs_copy(u, 0, step).wait_send()
            rs_copy(u, 1, step).wait_send()
        t_copy(u).wait_send()
        wd_out(u).wait()
        tot_copy(u).wait()
        tot_send(u).wait_send()
        tot_wait(u).wait_recv()

    @pl.loop(1, NZ)
    def _(d):
        dots_copy(d).wait_send()
        meta_copy(d).wait_send()

    gg_copy.wait()
    gg_ref[...] = ggx[0] + ggx[1]


def finish(
    tot, first_ref, second_ref, gain_ref, gates_in, wd_in,
    inv_ref, fg_ref, gg_ref, wd_ref,
):
    wd_ref[...] = wd_in[...]
    gg_ref[...] = gates_in[...]
    values = first_ref[...].astype(F32)
    inverse = lax.rsqrt(jnp.mean(values * values, axis=1, keepdims=True) + EPSILON)
    gain = gain_ref[...].astype(F32).reshape(1, WIDTH)
    along = jnp.zeros((TOK, 1), F32)
    for u in range(UNITS):
        cols = slice(u * FU, (u + 1) * FU)
        inv_ref[:, cols] = (second_ref[:, cols].astype(F32) - tot[0, u]).astype(BF)
        along = along + jnp.sum(tot[1, u] * gain[:, cols] * values[:, cols], axis=1, keepdims=True)
    shift = inverse * inverse * inverse * (along / WIDTH)
    for u in range(UNITS):
        cols = slice(u * FU, (u + 1) * FU)
        fg_ref[:, cols] = (
            inverse * (tot[1, u] * gain[:, cols]) - values[:, cols] * shift
        ).astype(BF)


def slot_tables():
    slot = np.arange(ROWS)
    owner = (slot[:, None] // SEG == np.arange(PLANE)[None, :]).astype(np.float32)
    block, order = slot % SEG // SHARE, slot % SHARE
    rank = np.where(block[:, None] == np.arange(NZ)[None, :], order[:, None], -100)
    return owner, rank.astype(np.float32)


def local(first, second, cot, gain, ids, gates, w_gate, w_up, w_down):
    owner, rank = slot_tables()
    vmem = pl.BlockSpec(memory_space=pltpu.VMEM)
    hbm = pl.BlockSpec(memory_space=pl.ANY)
    dma = pltpu.SemaphoreType.DMA
    tot, gg, wdg = pl.pallas_call(
        kernel,
        out_shape=(
            jax.ShapeDtypeStruct((2, UNITS, TOK, FU), F32),
            jax.ShapeDtypeStruct((TOP, TOK), F32),
            jax.ShapeDtypeStruct((HALF, WIDTH), BF),
        ),
        in_specs=[vmem] * 7 + [hbm] * 3,
        out_specs=(hbm, vmem, hbm),
        scratch_shapes=[
            pltpu.VMEM((WIDTH, FF), BF),
            pltpu.VMEM((WIDTH, FF), BF),
            pltpu.VMEM((FF, WIDTH), BF),
            pltpu.VMEM((2, UNITS, NZ, TOK, FU), BF),
            pltpu.VMEM((NZ, 2 * TOP, TOK), F32),
            pltpu.VMEM((ROWS, NZ * TOK), BF),
            pltpu.VMEM((NZ * TOK, ROWS), BF),
            pltpu.VMEM((ROWS, TOK), F32),
            pltpu.VMEM((UNITS, ROWS, FU), BF),
            pltpu.VMEM((UNITS, PLANE, SEG, 2 * FU), BF),
            pltpu.VMEM((UNITS, PLANE, SEG, 2 * FU), BF),
            pltpu.VMEM((UNITS, PLANE, SEG, 2 * FU), BF),
            pltpu.VMEM((3, ROWS, FF), F32),
            pltpu.VMEM((ROWS, FF), BF),
            pltpu.VMEM((FF, ROWS), BF),
            pltpu.VMEM((ROWS, FF), BF),
            pltpu.VMEM((ROWS, FF), BF),
            pltpu.VMEM((UNITS, 2, 4, TOK, FU), BF),
            pltpu.VMEM((UNITS, HALF, FU), BF),
            pltpu.VMEM((UNITS, HALF, FU), BF),
            pltpu.VMEM((ROWS, TOK), F32),
            pltpu.VMEM((NZ, PLANE, TOK), F32),
            pltpu.VMEM((NZ, PLANE, TOK), F32),
            pltpu.VMEM((2, TOP, TOK), F32),
            dma((3,)), dma((3,)), dma((3,)),
            dma((UNITS, 2, 4)), dma((UNITS, 2, 4)),
            dma((UNITS, 3)), dma((UNITS, 3)),
            dma((NZ,)), dma((NZ,)),
            dma((UNITS, PLANE)), dma((UNITS, PLANE)),
            dma((UNITS, PLANE)), dma((UNITS, PLANE)),
            dma((UNITS,)), dma((UNITS,)),
            dma((UNITS, 2, 4)), dma((UNITS, 2, 4)),
            dma((UNITS,)), dma((UNITS,)),
            dma((NZ,)), dma((NZ,)),
            dma((1,)), dma((1,)), dma((UNITS,)),
            dma((UNITS,)), dma((UNITS,)), dma((UNITS,)), pltpu.SemaphoreType.REGULAR,
        ],
        compiler_params=pltpu.CompilerParams(
            collective_id=1, has_side_effects=True, vmem_limit_bytes=63 << 20
        ),
        name="experts_backward",
    )(
        first, cot, gain, ids.T, gates.T,
        jnp.asarray(owner), jnp.asarray(rank), w_gate[0], w_up[0], w_down[0],
    )
    inv, fg, gg, wdg = pl.pallas_call(
        finish,
        out_shape=(
            jax.ShapeDtypeStruct((TOK, WIDTH), BF),
            jax.ShapeDtypeStruct((TOK, WIDTH), BF),
            jax.ShapeDtypeStruct((TOP, TOK), F32),
            jax.ShapeDtypeStruct((HALF, WIDTH), BF),
        ),
        in_specs=[vmem] * 6,
        out_specs=(vmem,) * 4,
        compiler_params=pltpu.CompilerParams(vmem_limit_bytes=62 << 20),
        name="streams",
    )(tot, first, second, gain, gg, wdg)
    return inv, fg, gg.T, wdg[None]


def solution(mesh):
    rows = P("ep", None)
    return jax.shard_map(
        local,
        mesh=mesh,
        in_specs=(
            rows, rows, rows, P(), rows, rows,
            P("ep", None, "rep"), P("ep", None, "rep"), P("ep", "rep", None),
        ),
        out_specs=(rows, rows, rows, P("ep", "rep", None)),
        check_vma=False,
    )
```
